32 devices in a mesh: energy: 2 (over x), momentum: 4 (over z), atom: 4 (over y, core).
Axes of the slice: x: 2, y: 2, z: 4, core: 2. Of those that a mesh axis runs over, the one named last changes fastest.
Arguments:
- green: bfloat16 [16, 32, 288, 256], P('momentum', 'atom', None, 'energy'), may hold values from -6 to 6
- neighbours: int32 [32, 8], P('atom'), may hold values from 0 to 31, as said below
- offsets: int32 [16], replicated, may hold values from 1 to 32, as said below
- emit_weight: bfloat16 [16, 16], replicated, may hold values from 0.0099487305 to 0.099609375
- absorb_weight: bfloat16 [16, 16], replicated, may hold values from 0.0099487305 to 0.099609375
- coupling: bfloat16 [32, 8, 12, 12], P('atom'), may hold values from -1.75 to 1.75
Outputs:
- selfenergy: float32 [16, 32, 288, 256], P('momentum', 'atom', None, 'energy')
The draws below stay inside these ranges and needn't reach their ends.
Inputs may be any that keep to these rules, and one draw needn't show every extreme that they name: `neighbours`: every entry lies within 2 of its own atom index, and some entry lies exactly 2 above it. `offsets`: all entries are distinct, and one of them equals 32.
All inputs are finite; a program needn't handle non-finite values.
Results may differ from the reference program's by a relative error of at most 0.0041.
Values may be sent and summed in bfloat16 or wider, within the bound.
No kernel may reach another device: no remote copies, remote signals or barrier semaphores. Data moves between devices by JAX's collectives and lax.ppermute only.
A program may use at most 128 MiB of HBM per device.

```python
import math
import jax
import jax.numpy as jnp
from jax import lax

ORB = 12
NB = 8
PHON = 16
SMAX = 32
REACH = 2
KPTS = 16
ATOMS = 32
ENERGIES = 256


def draw_neighbours(key, part):
    key_steps = jax.random.fold_in(key, 11)
    key_atom = jax.random.fold_in(key, 12)
    key_slot = jax.random.fold_in(key, 13)
    atom_ids = jnp.arange(ATOMS)[:, None]
    steps_drawn = jax.random.randint(key_steps, (ATOMS, NB), -REACH, REACH + 1)
    target = jnp.clip(atom_ids + steps_drawn, 0, ATOMS - 1)
    chosen_atom = jax.random.randint(key_atom, (), REACH, ATOMS - REACH)
    chosen_slot = jax.random.randint(key_slot, (), 0, NB)
    forced = (atom_ids == chosen_atom) & (jnp.arange(NB)[None, :] == chosen_slot)
    return jnp.where(forced, atom_ids + REACH, target).astype(jnp.int32)


def draw_offsets(key, part):
    key_order = jax.random.fold_in(key, 21)
    key_place = jax.random.fold_in(key, 22)
    ordering = jax.random.permutation(key_order, SMAX - 1) + 1
    values = jnp.concatenate([ordering[:PHON - 1], jnp.full((1,), SMAX, jnp.int32)])
    place = jax.random.randint(key_place, (), 0, PHON)
    return jnp.roll(values, place).astype(jnp.int32)


def shard_levels(rng, dims, cuts, least, high):
    level, own = 1.0, jax.random.fold_in(rng, 6)
    for position, blocks in cuts:
        heights = jnp.exp(jax.random.uniform(jax.random.fold_in(own, position), (blocks,), jnp.float32, least / len(cuts), high / len(cuts)))
        level = level * jnp.repeat(heights, dims[position] // blocks).reshape([-1 if axis == position else 1 for axis in range(len(dims))])
    return level


def bell_draw(rng, shape, scale, limit, split=(), dtype=jnp.bfloat16):
    values = jax.random.normal(rng, shape, jnp.float32) * scale
    if len(split) > 0:
        values = shard_levels(rng, shape, split, -0.22, 0.18) * values
    return jnp.clip(values, min=-limit, max=limit).astype(dtype)


def setup_inputs(seed: int = 0) -> dict:
    seeds = jax.random.split(jax.random.key(seed), 7)
    return {
        "green": bell_draw(seeds[0], (KPTS, ATOMS, 2 * ORB * ORB, ENERGIES), 1.0, 6.0, ((0, 4), (1, 4), (3, 2))),
        "neighbours": draw_neighbours(jax.random.fold_in(seeds[6], 71), 0),
        "offsets": draw_offsets(jax.random.fold_in(seeds[6], 71), 0),
        "emit_weight": jnp.clip(jnp.exp(jax.random.uniform(seeds[3], (PHON, KPTS), jnp.float32, math.log(0.0099487305), math.log(0.099609375))), 0.0099487305, 0.099609375).astype(jnp.bfloat16),
        "absorb_weight": jnp.clip(jnp.exp(jax.random.uniform(seeds[4], (PHON, KPTS), jnp.float32, math.log(0.0099487305), math.log(0.099609375))), 0.0099487305, 0.099609375).astype(jnp.bfloat16),
        "coupling": bell_draw(seeds[5], (ATOMS, NB, ORB, ORB), ORB ** -0.5, 1.75, ((0, 4),)),
    }


def reference(green, neighbours, offsets, emit_weight, absorb_weight, coupling):
    padded = jnp.pad(green.astype(jnp.float32), ((0, 0), (0, 0), (0, 0), (SMAX, SMAX)))
    lag_index = (jnp.arange(KPTS)[:, None] - jnp.arange(KPTS)[None, :]) % KPTS
    emit_full = emit_weight.astype(jnp.float32)
    absorb_full = absorb_weight.astype(jnp.float32)

    def add_mode(mode, running):
        shift = offsets[mode].astype(jnp.int32)
        early = lax.dynamic_slice_in_dim(padded, (SMAX - shift).astype(jnp.int32), ENERGIES, 3)
        later = lax.dynamic_slice_in_dim(padded, (SMAX + shift).astype(jnp.int32), ENERGIES, 3)
        emit_rows = emit_full[mode][lag_index]
        absorb_rows = absorb_full[mode][lag_index]
        running = running + jnp.einsum("pq,qaxe->paxe", emit_rows, early, precision=lax.Precision.HIGHEST)
        return running + jnp.einsum("pq,qaxe->paxe", absorb_rows, later, precision=lax.Precision.HIGHEST)

    hsum = lax.fori_loop(0, PHON, add_mode, jnp.zeros(green.shape, jnp.float32)).astype(jnp.bfloat16)
    blocks = hsum.reshape(KPTS, ATOMS, 2, ORB, ORB, ENERGIES)

    def add_slot(slot_index, accumulated):
        column = lax.dynamic_index_in_dim(neighbours, slot_index, 1, keepdims=False).astype(jnp.int32)
        chosen = jnp.take(blocks, column, axis=1).astype(jnp.float32)
        coupling_slot = lax.dynamic_index_in_dim(coupling, slot_index, 1, keepdims=False).astype(jnp.float32)
        half_block = jnp.einsum("aij,kacjle->kacile", coupling_slot, chosen).astype(jnp.bfloat16)
        return accumulated + jnp.einsum("kacile,ajl->kacije", half_block.astype(jnp.float32), coupling_slot)

    accumulated = lax.fori_loop(0, NB, add_slot, jnp.zeros(blocks.shape, jnp.float32))
    return accumulated.reshape(KPTS, ATOMS, 2 * ORB * ORB, ENERGIES)
```

```python
import functools

import jax
import jax.numpy as jnp
from jax import lax
from jax.experimental import pallas as pl
from jax.experimental.pallas import tpu as pltpu
from jax.sharding import PartitionSpec as P

SMAX = 32
REACH = 2
BF = jnp.bfloat16
F32 = jnp.float32
VMEM_LIMIT = 16 * 1024 * 1024
PACK_LIMIT = 16 * 1024 * 1024


def params(limit=VMEM_LIMIT):
    return pltpu.CompilerParams(vmem_limit_bytes=limit)


def smem():
    return pl.BlockSpec(memory_space=pltpu.SMEM)


def vmem():
    return pl.BlockSpec(memory_space=pltpu.VMEM)


def anywhere():
    return pl.BlockSpec(memory_space=pl.ANY)


def token():
    return jax.ShapeDtypeStruct((8, 128), F32)


def cost(flops, nbytes):
    return pl.CostEstimate(flops=0, bytes_accessed=0, transcendentals=0)


def atom_of(turn, atoms):
    return jnp.where(turn < REACH, turn, jnp.where(turn < 2 * REACH, turn + atoms - 2 * REACH, turn - REACH))


def pack_kernel(group, nz, z_ref, green, *refs):
    outs, sems = refs[-nz - 1:-1], refs[-1]
    atoms = green.shape[1]
    copies = []
    for r in range(nz):
        atom = atom_of(group * nz + lax.rem(z_ref[0] + r, nz), atoms)
        copies.append(pltpu.make_async_copy(green.at[:, atom], outs[r], sems.at[r]))
    for copy in copies:
        copy.start()
    for copy in copies:
        copy.wait()


def pack(z, green, nz, group, waits):
    k, _, comps, energies = green.shape
    piece = jax.ShapeDtypeStruct((k, comps, energies), BF)
    return pl.pallas_call(
        functools.partial(pack_kernel, group, nz),
        out_shape=(piece,) * nz,
        in_specs=[smem(), pl.BlockSpec(memory_space=pltpu.HBM)] + [vmem()] * len(waits),
        out_specs=(anywhere(),) * nz,
        scratch_shapes=[pltpu.SemaphoreType.DMA((nz,))],
        compiler_params=params(PACK_LIMIT),
        cost_estimate=cost(0, nz * piece.size * 4),
    )(z, green, *waits)


def halo_kernel(nz, sides, base_ref, *refs):
    pieces, outs = refs[:nz], refs[-sides:]
    k, rows, energies = pieces[0].shape
    lanes = k * SMAX
    row = lax.broadcasted_iota(jnp.int32, (energies, lanes), 0)
    col = lax.broadcasted_iota(jnp.int32, (energies, lanes), 1)
    for side in range(sides):
        picks = [(row - base_ref[side] == col - kk * SMAX) & (col >= kk * SMAX) & (col < (kk + 1) * SMAX) for kk in range(k)]
        pick = jnp.concatenate([jnp.where(p, 1.0, 0.0) for p in picks], axis=0).astype(BF)
        for r in range(nz):
            wide = jnp.concatenate([pieces[r][kk] for kk in range(k)], axis=1)
            outs[side][r] = jnp.dot(wide, pick, preferred_element_type=F32).astype(BF)


def halo_pack(base, pieces, sides, waits):
    nz = len(pieces)
    k, rows, energies = pieces[0].shape
    out = jax.ShapeDtypeStruct((nz, rows, k * SMAX), BF)
    return pl.pallas_call(
        functools.partial(halo_kernel, nz, sides),
        out_shape=(out,) * sides,
        in_specs=[smem()] + [vmem()] * nz + [vmem()] * len(waits),
        out_specs=(vmem(),) * sides,
        compiler_params=params(),
        cost_estimate=cost(2 * sides * out.size * k * energies, nz * pieces[0].size * 2),
    )(base, *pieces, *waits)


def table_kernel(nz, k, energies, sides, off_ref, emit_ref, absorb_ref, pos_ref, *refs):
    main, halos, done, own, edge = refs[0], refs[1:1 + sides], refs[1 + sides], refs[2 + sides], refs[3 + sides]
    done[...] = jnp.zeros_like(done)
    phonons = off_ref.shape[0]
    total = nz * k
    pairs = total // 2

    def lag_matrix(lag, sources, first):
        distance = lax.broadcasted_iota(jnp.int32, (sources, energies), 1) - lax.broadcasted_iota(jnp.int32, (sources, energies), 0) - first
        value = jnp.zeros((sources, energies), F32)
        for w in range(phonons):
            value = jnp.where(distance == off_ref[w], emit_ref[w, lag], value)
            value = jnp.where(distance == -off_ref[w], absorb_ref[w, lag], value)
        return value.astype(BF)

    def step(lag, carry):
        own[lag] = lag_matrix(lag, energies, 0)
        for side in range(sides):
            edge[side, lag] = lag_matrix(lag, SMAX, pos_ref[side])
        return carry

    lax.fori_loop(0, total, step, 0)
    for i in range(2 * pairs - 1):
        m = 2 * (pairs - 1 - i)
        for a in range(2):
            for b in range(2):
                at = i * 2 * energies + a * energies
                main[at:at + energies, b * energies:(b + 1) * energies] = own[(m + b - a) % total]
    per = k // 2
    for side in range(sides):
        for par in range(per):
            for i in range(2 * nz - 1):
                m = 2 * (per * (nz - 1 - i) + par)
                for a in range(k):
                    for b in range(2):
                        at = i * k * SMAX + a * SMAX
                        halos[side][par, at:at + SMAX, b * energies:(b + 1) * energies] = edge[side, (m + b - a) % total]


def tables(offsets, emit, absorb, pos, nz, k, energies):
    sides = pos.shape[0]
    total = nz * k
    main = jax.ShapeDtypeStruct(((total - 1) * 2 * energies, 2 * energies), BF)
    halo = jax.ShapeDtypeStruct((k // 2, (2 * nz - 1) * k * SMAX, 2 * energies), BF)
    return pl.pallas_call(
        functools.partial(table_kernel, nz, k, energies, sides),
        out_shape=(main,) + (halo,) * sides + (token(),),
        in_specs=[smem()] * 4,
        out_specs=(vmem(),) * (2 + sides),
        scratch_shapes=[pltpu.VMEM((total, energies, energies), BF), pltpu.VMEM((sides, total, SMAX, energies), BF)],
        compiler_params=params(),
        cost_estimate=cost(total * energies * energies * 100, main.size * 2),
    )(offsets, emit.astype(F32), absorb.astype(F32), pos)


def sum_kernel(nz, sides, *refs):
    pieces, refs = refs[:nz], refs[nz:]
    halos, refs = refs[:sides], refs[sides:]
    main, refs = refs[0], refs[1:]
    edges, refs = refs[:sides], refs[sides:]
    outs, done, wide = refs[-nz - 2:-2], refs[-2], refs[-1]
    done[...] = jnp.zeros_like(done)
    k, rows, energies = pieces[0].shape
    total = nz * k
    pairs = total // 2
    per = k // 2
    strip = k * SMAX
    inner = total * energies
    for q in range(nz):
        piece = pieces[(nz - q) % nz]
        for kk in range(k):
            wide[:, (q * k + kk) * energies:(q * k + kk + 1) * energies] = piece[kk]
        for side in range(sides):
            at = inner + (side * nz + q) * strip
            wide[:, at:at + strip] = halos[side][(nz - q) % nz]
    for pair in range(pairs):
        top = (pairs - 1 - pair) * 2 * energies
        value = jnp.dot(wide[:, :inner], main[top:top + inner, :], preferred_element_type=F32)
        for side in range(sides):
            at = inner + side * nz * strip
            start = (nz - 1 - pair // per) * strip
            value += jnp.dot(wide[:, at:at + nz * strip], edges[side][pair % per, start:start + nz * strip, :], preferred_element_type=F32)
        value = value.astype(BF)
        for b in range(2):
            outs[pair // per][2 * (pair % per) + b] = value[:, b * energies:(b + 1) * energies]


def phonon_sum(pieces, halos, main, edges, waits):
    nz, sides = len(pieces), len(halos)
    k, rows, energies = pieces[0].shape
    out = jax.ShapeDtypeStruct((k, rows, energies), BF)
    depth = nz * k * energies + sides * nz * k * SMAX
    return pl.pallas_call(
        functools.partial(sum_kernel, nz, sides),
        out_shape=(out,) * nz + (token(),),
        in_specs=[vmem()] * (nz + sides + 1 + sides + len(waits)),
        out_specs=(vmem(),) * (nz + 1),
        scratch_shapes=[pltpu.VMEM((rows, depth), BF)],
        compiler_params=params(),
        cost_estimate=cost(2 * rows * depth * nz * k * energies, main.size * 2),
    )(*pieces, *halos, main, *edges, *waits)


def coupling_kernel(slots, nz, inner_atoms, atoms, skip, z_ref, near_ref, c_ref, rows_a, rows_b, cols_a, cols_b, place, _, outer, inner, done, total):
    atom = pl.program_id(0) + skip
    done[...] = jnp.zeros_like(done)
    blocks = c_ref[0]
    left = jnp.dot(blocks, cols_a[...], preferred_element_type=F32).astype(BF)
    right = jnp.dot(blocks, cols_b[...], preferred_element_type=F32).astype(BF)
    total[...] = jnp.zeros_like(total)
    for n in range(slots):
        product = jnp.dot(rows_a[n], left, preferred_element_type=F32) * jnp.dot(rows_b[n], right, preferred_element_type=F32)
        total[near_ref[atom, n] + atom] += product
    first = jnp.where(atom < 2 * REACH, 0, atoms)
    value = jnp.dot(total[first].astype(BF), place[0], preferred_element_type=F32)
    for i in range(1, 2 * REACH):
        value += jnp.dot(total[first + i].astype(BF), place[i], preferred_element_type=F32)
    outer[0] = value.astype(BF)
    value = None
    for i in range(inner_atoms):
        turn = 2 * REACH + i // nz * nz + lax.rem(z_ref[0] + nz - i % nz, nz)
        term = jnp.dot(total[turn].astype(BF), place[i], preferred_element_type=F32)
        value = term if value is None else value + term
    inner[0] = value.astype(BF)


def coupling_matrices(z, nz, near, coupling, skip, count, wait):
    atoms, slots, orb, _ = coupling.shape
    comp = orb * orb
    inner_atoms = atoms - 2 * REACH
    blocks = coupling.reshape(atoms, slots * orb, orb)
    row = jnp.arange(comp)
    source = jnp.arange(slots * orb)
    slot = jnp.arange(slots)[:, None, None]
    rows_a = (source[None, None, :] == slot * orb + (row // orb)[None, :, None]).astype(BF)
    rows_b = (source[None, None, :] == slot * orb + (row % orb)[None, :, None]).astype(BF)
    cols_a = (jnp.arange(orb)[:, None] == (row // orb)[None, :]).astype(BF)
    cols_b = (jnp.arange(orb)[:, None] == (row % orb)[None, :]).astype(BF)
    wide = max(2 * REACH, inner_atoms)
    place = (jnp.arange(wide * comp)[None, None, :] == jnp.arange(wide)[:, None, None] * comp + row[None, :, None]).astype(BF)

    def fixed(array):
        return pl.BlockSpec(array.shape, lambda a: (0,) * len(array.shape))

    fixed_arrays = (rows_a, rows_b, cols_a, cols_b, place)
    out = jax.ShapeDtypeStruct((count, comp, wide * comp), BF)
    out_spec = pl.BlockSpec((1, comp, wide * comp), lambda a: (a, 0, 0))
    return pl.pallas_call(
        functools.partial(coupling_kernel, slots, nz, inner_atoms, atoms, skip),
        grid=(count,),
        out_shape=(out, out, token()),
        in_specs=[smem(), smem(), pl.BlockSpec((1, slots * orb, orb), lambda a: (a + skip, 0, 0))] + [fixed(v) for v in fixed_arrays + (wait,)],
        out_specs=(out_spec, out_spec, fixed(token())),
        scratch_shapes=[pltpu.VMEM((atoms + 2 * REACH, comp, comp), F32)],
        compiler_params=params(),
        cost_estimate=cost(atoms * comp * comp * slots * 400, atoms * comp * comp * 16),
    )(z, near, blocks, *fixed_arrays, wait)


def edge_kernel(nz, z_ref, *refs):
    pieces, low, high = refs[:nz], refs[-2], refs[-1]
    for r in range(nz):
        turn = lax.rem(z_ref[0] + nz - r, nz)
        for j in range(2 * REACH):
            target = low if j < REACH else high

            @pl.when(turn == j)
            def _(r=r, j=j, target=target):
                target[j % REACH] = pieces[r][...]


def edge_pack(z, pieces, waits):
    nz = len(pieces)
    out = jax.ShapeDtypeStruct((REACH,) + pieces[0].shape, BF)
    return pl.pallas_call(
        functools.partial(edge_kernel, nz),
        out_shape=(out, out),
        in_specs=[smem()] + [vmem()] * nz + [vmem()] * len(waits),
        out_specs=(vmem(), vmem()),
        compiler_params=params(),
        cost_estimate=cost(0, nz * pieces[0].size * 4),
    )(z, *pieces, *waits)


def arrive_kernel(*refs):
    refs[-1][...] = jnp.zeros_like(refs[-1])


def arrive(pieces):
    return pl.pallas_call(
        arrive_kernel,
        out_shape=token(),
        in_specs=[vmem()] * len(pieces),
        out_specs=vmem(),
        compiler_params=params(),
        cost_estimate=pl.CostEstimate(flops=40 * 10**9, bytes_accessed=0, transcendentals=0),
    )(*[piece[0, :16] for piece in pieces])


def apply_kernel(before, low, high, after, *refs):
    pieces, (outer_low, outer_high, inner_low, inner_high, _, out) = refs[:-6], refs[-6:]
    _, atoms, comp, energies = out.shape
    edge = 2 * REACH * comp
    half = inner_low.shape[0]
    rows = pl.ds(pl.multiple_of(pl.program_id(0) * comp, 16), comp)
    k = pl.program_id(1) * 2

    def window(refs):
        return jnp.concatenate([jnp.concatenate([r[k, rows, :], r[k + 1, rows, :]], axis=1) for r in refs], axis=0)

    def put(value, first):
        for a in range(value.shape[0] // comp):
            for b in range(2):
                out[b, first + a] = value[a * comp:(a + 1) * comp, b * energies:(b + 1) * energies]

    inside = window(pieces)
    value = jnp.dot(inner_low[:, :inside.shape[0]], inside, preferred_element_type=F32)
    value_edge = jnp.dot(outer_low[:edge, :edge], window([before.at[0], before.at[1], low.at[0], low.at[1]]), preferred_element_type=F32)
    put(value[:edge] + value_edge, 0)
    if half > edge:
        put(value[edge:], 2 * REACH)
    value = jnp.dot(inner_high[:, :inside.shape[0]], inside, preferred_element_type=F32)
    value_edge = jnp.dot(outer_high[half - edge:, :edge], window([high.at[0], high.at[1], after.at[0], after.at[1]]), preferred_element_type=F32)
    if half > edge:
        put(value[:half - edge], atoms // 2)
    put(value[half - edge:] + value_edge, atoms - 2 * REACH)


def apply_couplings(before, low, high, after, pieces, outers, inners, wait, shape):
    k, atoms, comps, energies = shape
    comp = comps // 2
    matrices = [m.reshape(-1, m.shape[2]) for m in (*outers, *inners)]
    return pl.pallas_call(
        apply_kernel,
        grid=(2, k // 2),
        out_shape=jax.ShapeDtypeStruct(shape, F32),
        in_specs=[vmem()] * (4 + len(pieces) + len(matrices) + 1),
        out_specs=pl.BlockSpec((2, atoms, comp, energies), lambda c, kk: (kk, 0, c, 0)),
        compiler_params=params(),
        cost_estimate=cost(0, 0),
    )(before, low, high, after, *pieces, *matrices, wait)


def shards(green, neighbours, offsets, emit_weight, absorb_weight, coupling):
    k, atoms, comps, energies = green.shape
    nz, ne, ny = (lax.axis_size(axis) for axis in ("momentum", "energy", "atom"))
    groups = atoms // nz
    z = lax.axis_index("momentum").astype(jnp.int32).reshape(1)
    where_e = lax.axis_index("energy").astype(jnp.int32)

    def around(array, r):
        return lax.ppermute(array, "momentum", [(i, (i + r) % nz) for i in range(nz)])

    if ne == 2:
        base = jnp.where(where_e == 0, energies - SMAX, 0).reshape(1)
        pos = jnp.where(where_e == 0, energies, -SMAX).reshape(1)
        routes = [[(0, 1), (1, 0)]]
    else:
        base = jnp.array([energies - SMAX, 0], jnp.int32)
        pos = jnp.array([-SMAX, energies], jnp.int32)
        routes = [[(i, i + 1) for i in range(ne - 1)], [(i + 1, i) for i in range(ne - 1)]]
    sides = len(routes)

    def send(group, *waits):
        sent = [lax.dynamic_index_in_dim(green, atom_of(group * nz + lax.rem(z[0] + r, nz), atoms), 1, keepdims=False) for r in range(nz)]
        if waits:
            sent = list(lax.optimization_barrier((sent, waits))[0])
        return spread(sent, ([[1, 2, 3], [1, 2, 3], [1, 2, 3], [1, 2, 3]])[group])

    def spread(sent, order):
        there = {r: around(sent[r], r) for r in order}
        return [sent[0]] + [there[r] for r in range(1, nz)]

    got = [send(0)]
    main, *edges, done = tables(offsets, emit_weight, absorb_weight, pos, nz, k, energies)
    first = lax.axis_index("atom") * atoms
    near = neighbours - (first + jnp.arange(atoms))[:, None].astype(jnp.int32) + REACH
    half = atoms // 2
    outer_low, inner_low, done = coupling_matrices(z, nz, near, coupling, 0, half, done)
    for group in range(1, groups):
        got.append(send(group, done))
    outer_high, inner_high, done = coupling_matrices(z, nz, near, coupling, half, half, done)

    waits = [done]
    back = []
    for group in range(groups):
        halos = halo_pack(base, got[group], sides, waits)
        halos = [jnp.concatenate([lax.ppermute(h[i:i + 2], "energy", route) for i in range(0, nz, 2)]) for h, route in zip(halos, routes)]
        *sums, sum_done = phonon_sum(got[group], halos, main, edges, [back[-1][2][0, :16]] if back else [])
        waits = [sum_done]
        back.append(spread(sums, ([[1, 2, 3], [1, 2, 3], [1, 2, 3], [1, 2, 3]])[2 + group]))

    low, high = edge_pack(z, back[0], waits)
    after = lax.ppermute(low, "atom", [(i + 1, i) for i in range(ny - 1)])
    before = lax.ppermute(high, "atom", [(i, i + 1) for i in range(ny - 1)])
    pieces = [piece for group in back[1:] for piece in group]
    return apply_couplings(before, low, high, after, pieces, (outer_low, outer_high), (inner_low, inner_high), arrive([p for group in back[1:] for p in group[1:]]), green.shape)


def solution(mesh):
    in_specs = (
        P("momentum", "atom", None, "energy"),
        P("atom", None),
        P(),
        P(),
        P(),
        P("atom", None, None, None),
    )
    out_specs = P("momentum", "atom", None, "energy")
    return jax.shard_map(shards, mesh=mesh, in_specs=in_specs, out_specs=out_specs, check_vma=False)
```

```python
import functools

import jax
import jax.numpy as jnp
from jax import lax
from jax.experimental import pallas as pl
from jax.experimental.pallas import tpu as pltpu
from jax.sharding import PartitionSpec as P

SMAX = 32
REACH = 2
BF = jnp.bfloat16
F32 = jnp.float32
VMEM_LIMIT = 16 * 1024 * 1024
PACK_LIMIT = 62 * 1024 * 1024


def params(limit=VMEM_LIMIT):
    return pltpu.CompilerParams(vmem_limit_bytes=limit)


def smem():
    return pl.BlockSpec(memory_space=pltpu.SMEM)


def vmem():
    return pl.BlockSpec(memory_space=pltpu.VMEM)


def anywhere():
    return pl.BlockSpec(memory_space=pl.ANY)


def token():
    return jax.ShapeDtypeStruct((8, 128), F32)


def cost(flops, nbytes):
    return pl.CostEstimate(flops=0, bytes_accessed=0, transcendentals=0)


def atom_of(turn, atoms):
    return jnp.where(turn < REACH, turn, jnp.where(turn < 2 * REACH, turn + atoms - 2 * REACH, turn - REACH))


def pack_kernel(group, nz, ids, green, *refs):
    outs, sems = refs[-nz - 1:-1], refs[-1]
    atoms = green.shape[1]
    copies = []
    for r in range(nz):
        atom = atom_of(group * nz + lax.rem(ids[0] + r, nz), atoms)
        copies.append(pltpu.make_async_copy(green.at[:, atom], outs[r], sems.at[r]))
    for copy in copies:
        copy.start()
    for copy in copies:
        copy.wait()


def pack(ids, green, nz, group, waits):
    k, _, comps, energies = green.shape
    piece = jax.ShapeDtypeStruct((k, comps, energies), BF)
    return pl.pallas_call(
        functools.partial(pack_kernel, group, nz),
        out_shape=(piece,) * nz,
        in_specs=[smem(), pl.BlockSpec(memory_space=pltpu.HBM)] + [vmem()] * len(waits),
        out_specs=(anywhere(),) * nz,
        scratch_shapes=[pltpu.SemaphoreType.DMA((nz,))],
        compiler_params=params(VMEM_LIMIT if waits else PACK_LIMIT),
        cost_estimate=cost(0, nz * piece.size * 4),
    )(ids, green, *waits)


def own_edge(place, side, sides, energies):
    last = place == 0 if sides == 1 else side == 0
    return jnp.where(last, energies - SMAX, 0)


def far_edge(place, side, sides, energies):
    above = place == 0 if sides == 1 else side == 1
    return jnp.where(above, energies, -SMAX)


def halo_kernel(nz, sides, ids, *refs):
    pieces, outs = refs[:nz], refs[-2 * sides:]
    half = nz // 2
    k, rows, energies = pieces[0].shape
    lanes = k * SMAX
    row = lax.broadcasted_iota(jnp.int32, (energies, lanes), 0)
    col = lax.broadcasted_iota(jnp.int32, (energies, lanes), 1)
    for side in range(sides):
        base = own_edge(ids[1], side, sides, energies)
        picks = [(row - base == col - kk * SMAX) & (col >= kk * SMAX) & (col < (kk + 1) * SMAX) for kk in range(k)]
        pick = jnp.concatenate([jnp.where(p, 1.0, 0.0) for p in picks], axis=0).astype(BF)
        for r in range(nz):
            wide = jnp.concatenate([pieces[r][kk] for kk in range(k)], axis=1)
            outs[2 * side + r // half][r % half] = jnp.dot(wide, pick, preferred_element_type=F32).astype(BF)


def halo_pack(ids, pieces, sides, waits):
    nz = len(pieces)
    k, rows, energies = pieces[0].shape
    out = jax.ShapeDtypeStruct((nz // 2, rows, k * SMAX), BF)
    return pl.pallas_call(
        functools.partial(halo_kernel, nz, sides),
        out_shape=(out,) * (2 * sides),
        in_specs=[smem()] + [vmem()] * nz + [anywhere()] * len(waits),
        out_specs=(vmem(),) * (2 * sides),
        compiler_params=params(),
        cost_estimate=cost(2 * sides * out.size * k * energies, nz * pieces[0].size * 2),
    )(ids, *pieces, *waits)


def table_kernel(nz, k, energies, sides, off_ref, emit_ref, absorb_ref, ids, *refs):
    main, halos, done, own, edge = refs[0], refs[1:1 + sides], refs[1 + sides], refs[2 + sides], refs[3 + sides]
    done[...] = jnp.zeros_like(done)
    phonons = off_ref.shape[0]
    total = nz * k
    pairs = total // 2

    def lag_matrix(lag, sources, first):
        distance = lax.broadcasted_iota(jnp.int32, (sources, energies), 1) - lax.broadcasted_iota(jnp.int32, (sources, energies), 0) - first
        value = jnp.zeros((sources, energies), F32)
        for w in range(phonons):
            value = jnp.where(distance == off_ref[w], emit_ref[w, lag], value)
            value = jnp.where(distance == -off_ref[w], absorb_ref[w, lag], value)
        return value.astype(BF)

    def step(lag, carry):
        own[lag] = lag_matrix(lag, energies, 0)
        for side in range(sides):
            edge[side, lag] = lag_matrix(lag, SMAX, far_edge(ids[1], side, sides, energies))
        return carry

    lax.fori_loop(0, total, step, 0)
    for i in range(2 * pairs - 1):
        m = 2 * (pairs - 1 - i)
        for a in range(2):
            for b in range(2):
                at = i * 2 * energies + a * energies
                main[at:at + energies, b * energies:(b + 1) * energies] = own[(m + b - a) % total]
    per = k // 2
    for side in range(sides):
        for par in range(per):
            for i in range(2 * nz - 1):
                m = 2 * (per * (nz - 1 - i) + par)
                for a in range(k):
                    for b in range(2):
                        at = i * k * SMAX + a * SMAX
                        halos[side][par, at:at + SMAX, b * energies:(b + 1) * energies] = edge[side, (m + b - a) % total]


def tables(offsets, emit, absorb, ids, sides, nz, k, energies):
    total = nz * k
    main = jax.ShapeDtypeStruct(((total - 1) * 2 * energies, 2 * energies), BF)
    halo = jax.ShapeDtypeStruct((k // 2, (2 * nz - 1) * k * SMAX, 2 * energies), BF)
    return pl.pallas_call(
        functools.partial(table_kernel, nz, k, energies, sides),
        out_shape=(main,) + (halo,) * sides + (token(),),
        in_specs=[smem()] * 4,
        out_specs=(vmem(),) * (2 + sides),
        scratch_shapes=[pltpu.VMEM((total, energies, energies), BF), pltpu.VMEM((sides, total, SMAX, energies), BF)],
        compiler_params=params(),
        cost_estimate=cost(total * energies * energies * 100, main.size * 2),
    )(offsets, emit.astype(F32), absorb.astype(F32), ids)


def sum_kernel(nz, sides, *refs):
    pieces, refs = refs[:nz], refs[nz:]
    halos, refs = refs[:2 * sides], refs[2 * sides:]
    main, refs = refs[0], refs[1:]
    edges, refs = refs[:sides], refs[sides:]
    outs, done, wide = refs[-nz - 2:-2], refs[-2], refs[-1]
    done[...] = jnp.zeros_like(done)
    k, rows, energies = pieces[0].shape
    total = nz * k
    pairs = total // 2
    per = k // 2
    strip = k * SMAX
    inner = total * energies
    for q in range(nz):
        piece = pieces[(nz - q) % nz]
        for kk in range(k):
            wide[:, (q * k + kk) * energies:(q * k + kk + 1) * energies] = piece[kk]
        for side in range(sides):
            at = inner + (side * nz + q) * strip
            r = (nz - q) % nz
            wide[:, at:at + strip] = halos[2 * side + r // (nz // 2)][r % (nz // 2)]
    for pair in range(pairs):
        top = (pairs - 1 - pair) * 2 * energies
        value = jnp.dot(wide[:, :inner], main[top:top + inner, :], preferred_element_type=F32)
        for side in range(sides):
            at = inner + side * nz * strip
            start = (nz - 1 - pair // per) * strip
            value += jnp.dot(wide[:, at:at + nz * strip], edges[side][pair % per, start:start + nz * strip, :], preferred_element_type=F32)
        value = value.astype(BF)
        for b in range(2):
            outs[pair // per][2 * (pair % per) + b] = value[:, b * energies:(b + 1) * energies]


def phonon_sum(pieces, halos, main, edges, waits):
    nz, sides = len(pieces), len(halos) // 2
    k, rows, energies = pieces[0].shape
    out = jax.ShapeDtypeStruct((k, rows, energies), BF)
    depth = nz * k * energies + sides * nz * k * SMAX
    return pl.pallas_call(
        functools.partial(sum_kernel, nz, sides),
        out_shape=(out,) * nz + (token(),),
        in_specs=[vmem()] * (nz + 2 * sides + 1 + sides) + [anywhere()] * len(waits),
        out_specs=(vmem(),) * (nz + 1),
        scratch_shapes=[pltpu.VMEM((rows, depth), BF)],
        compiler_params=params(),
        cost_estimate=cost(2 * rows * depth * nz * k * energies, main.size * 2),
    )(*pieces, *halos, main, *edges, *waits)


def coupling_kernel(slots, nz, inner_atoms, atoms, skip, ids, near_ref, c_ref, wait, outer, inner, done, total):
    atom = pl.program_id(0) + skip
    done[...] = jnp.zeros_like(done)
    blocks = c_ref[0]
    depth, orb = blocks.shape
    comp = total.shape[1]

    def iotas(rows, cols):
        return lax.broadcasted_iota(jnp.int32, (rows, cols), 0), lax.broadcasted_iota(jnp.int32, (rows, cols), 1)

    def picks(condition):
        return jnp.where(condition, 1.0, 0.0).astype(BF)

    def over(index):
        return lax.shift_right_logical(index * (4096 // orb + 1), 12)

    row, col = iotas(orb, comp)
    left = jnp.dot(blocks, picks(row == over(col)), preferred_element_type=F32).astype(BF)
    right = jnp.dot(blocks, picks(row == col - over(col) * orb), preferred_element_type=F32).astype(BF)
    total[...] = jnp.zeros_like(total)
    row, col = iotas(comp, depth)
    for n in range(slots):
        spread_left = jnp.dot(picks(col == over(row) * slots + n), left, preferred_element_type=F32)
        spread_right = jnp.dot(picks(col == (row - over(row) * orb) * slots + n), right, preferred_element_type=F32)
        total[near_ref[atom, n] - ids[2] + REACH] += spread_left * spread_right

    def side_by_side(indices, width):
        row, col = iotas(comp, width)
        value = None
        for i, index in enumerate(indices):
            term = jnp.dot(total[index].astype(BF), picks(col == row + i * comp), preferred_element_type=F32)
            value = term if value is None else value + term
        return value.astype(BF)

    start = jnp.where(atom < 2 * REACH, 0, atoms)
    outer[0] = side_by_side([start + i for i in range(2 * REACH)], outer.shape[2])
    turns = [2 * REACH + i // nz * nz + lax.rem(ids[0] + nz - i % nz, nz) for i in range(inner_atoms)]
    inner[0] = side_by_side(turns, inner.shape[2])


def coupling_matrices(ids, nz, neighbours, coupling, skip, count, wait):
    atoms, slots, orb, _ = coupling.shape
    comp = orb * orb
    inner_atoms = atoms - 2 * REACH
    blocks = jnp.transpose(coupling, (0, 2, 1, 3)).reshape(atoms, orb * slots, orb)

    def out(blocks_wide):
        return jax.ShapeDtypeStruct((count, comp, blocks_wide * comp), BF), pl.BlockSpec((1, comp, blocks_wide * comp), lambda a: (a, 0, 0))

    outer, outer_spec = out(2 * REACH)
    inner, inner_spec = out(inner_atoms)
    done_spec = pl.BlockSpec(token().shape, lambda a: (0, 0))
    return pl.pallas_call(
        functools.partial(coupling_kernel, slots, nz, inner_atoms, atoms, skip),
        grid=(count,),
        out_shape=(outer, inner, token()),
        in_specs=[smem(), smem(), pl.BlockSpec((1, orb * slots, orb), lambda a: (a + skip, 0, 0)), anywhere()],
        out_specs=(outer_spec, inner_spec, done_spec),
        scratch_shapes=[pltpu.VMEM((atoms + 2 * REACH, comp, comp), F32)],
        compiler_params=params(),
        cost_estimate=cost(0, 0),
    )(ids, neighbours, blocks, wait)


def edge_kernel(nz, ids, *refs):
    pieces, low, high = refs[:nz], refs[-2], refs[-1]
    for r in range(nz):
        turn = lax.rem(ids[0] + nz - r, nz)
        for j in range(2 * REACH):
            target = low if j < REACH else high

            @pl.when(turn == j)
            def _(r=r, j=j, target=target):
                target[j % REACH] = pieces[r][...]


def edge_pack(ids, pieces, waits):
    nz = len(pieces)
    out = jax.ShapeDtypeStruct((REACH,) + pieces[0].shape, BF)
    return pl.pallas_call(
        functools.partial(edge_kernel, nz),
        out_shape=(out, out),
        in_specs=[smem()] + [vmem()] * nz + [anywhere()] * len(waits),
        out_specs=(vmem(), vmem()),
        compiler_params=params(),
        cost_estimate=cost(0, nz * pieces[0].size * 4),
    )(ids, *pieces, *waits)


def arrive_kernel(*refs):
    refs[-1][...] = jnp.zeros_like(refs[-1])


def arrive(pieces):
    return pl.pallas_call(
        arrive_kernel,
        out_shape=token(),
        in_specs=[anywhere()] * len(pieces),
        out_specs=vmem(),
        compiler_params=params(),
        cost_estimate=pl.CostEstimate(flops=40 * 10**9, bytes_accessed=0, transcendentals=0),
    )(*pieces)


def apply_kernel(before, low, high, after, *refs):
    pieces, (outer_low, outer_high, inner_low, inner_high, _, out) = refs[:-6], refs[-6:]
    _, atoms, comp, energies = out.shape
    edge = 2 * REACH * comp
    half = inner_low.shape[0]
    rows = pl.ds(pl.multiple_of(pl.program_id(0) * comp, 16), comp)
    k = pl.program_id(1) * 2

    def window(refs):
        return jnp.concatenate([jnp.concatenate([r[k, rows, :], r[k + 1, rows, :]], axis=1) for r in refs], axis=0)

    def put(value, first):
        for a in range(value.shape[0] // comp):
            for b in range(2):
                out[b, first + a] = value[a * comp:(a + 1) * comp, b * energies:(b + 1) * energies]

    inside = window(pieces)
    value = jnp.dot(inner_low[:, :inside.shape[0]], inside, preferred_element_type=F32)
    value_edge = jnp.dot(outer_low[:edge, :edge], window([before.at[0], before.at[1], low.at[0], low.at[1]]), preferred_element_type=F32)
    put(value[:edge] + value_edge, 0)
    if half > edge:
        put(value[edge:], 2 * REACH)
    value = jnp.dot(inner_high[:, :inside.shape[0]], inside, preferred_element_type=F32)
    value_edge = jnp.dot(outer_high[half - edge:, :edge], window([high.at[0], high.at[1], after.at[0], after.at[1]]), preferred_element_type=F32)
    if half > edge:
        put(value[:half - edge], atoms // 2)
    put(value[half - edge:] + value_edge, atoms - 2 * REACH)


def apply_couplings(before, low, high, after, pieces, outers, inners, wait, shape):
    k, atoms, comps, energies = shape
    comp = comps // 2
    matrices = [m.reshape(-1, m.shape[2]) for m in (*outers, *inners)]
    return pl.pallas_call(
        apply_kernel,
        grid=(2, k // 2),
        out_shape=jax.ShapeDtypeStruct(shape, F32),
        in_specs=[vmem()] * (4 + len(pieces) + len(matrices) + 1),
        out_specs=pl.BlockSpec((2, atoms, comp, energies), lambda c, kk: (kk, 0, c, 0)),
        compiler_params=params(),
        cost_estimate=cost(0, 0),
    )(before, low, high, after, *pieces, *matrices, wait)


def shards(green, neighbours, offsets, emit_weight, absorb_weight, coupling):
    k, atoms, comps, energies = green.shape
    nz, ne, ny = (lax.axis_size(axis) for axis in ("momentum", "energy", "atom"))
    groups = atoms // nz
    ids = jnp.stack([lax.axis_index("momentum"), lax.axis_index("energy"), lax.axis_index("atom") * atoms]).astype(jnp.int32)
    green, ids = lax.optimization_barrier((green, ids))

    def around(array, r):
        return lax.ppermute(array, "momentum", [(i, (i + r) % nz) for i in range(nz)])

    if ne == 2:
        routes = [[(0, 1), (1, 0)]]
    else:
        routes = [[(i, i + 1) for i in range(ne - 1)], [(i + 1, i) for i in range(ne - 1)]]
    sides = len(routes)

    def send(group, *waits):
        if group == 0:
            sent = [lax.dynamic_index_in_dim(green, atom_of(group * nz + lax.rem(ids[0] + r, nz), atoms), 1, keepdims=False) for r in range(nz)]
        else:
            sent = pack(ids, green, nz, group, waits)
        return spread(sent, ([[1, 2, 3], [1, 2, 3], [1, 2, 3], [1, 2, 3]])[group])

    def spread(sent, order):
        there = {r: around(sent[r], r) for r in order}
        return [sent[0]] + [there[r] for r in range(1, nz)]

    got = [send(0)]
    main, *edges, done = tables(offsets, emit_weight, absorb_weight, ids, sides, nz, k, energies)
    half = atoms // 2
    outer_low, inner_low, done = coupling_matrices(ids, nz, neighbours, coupling, 0, half, done)
    for group in range(1, groups):
        got.append(send(group, done))
    outer_high, inner_high, done = coupling_matrices(ids, nz, neighbours, coupling, half, half, done)

    waits = [done]
    back = []
    for group in range(groups):
        halos = halo_pack(ids, got[group], sides, waits)
        halos = [lax.ppermute(h, "energy", routes[i // 2]) for i, h in enumerate(halos)]
        *sums, sum_done = phonon_sum(got[group], halos, main, edges, [back[-1][r] for r in [2]] if back else [])
        waits = [sum_done]
        back.append(spread(sums, ([[1, 2, 3], [1, 2, 3], [1, 2, 3], [1, 2, 3]])[2 + group]))

    low, high = edge_pack(ids, back[0], waits)
    after = lax.ppermute(low, "atom", [(i + 1, i) for i in range(ny - 1)])
    before = lax.ppermute(high, "atom", [(i, i + 1) for i in range(ny - 1)])
    pieces = [piece for group in back[1:] for piece in group]
    return apply_couplings(before, low, high, after, pieces, (outer_low, outer_high), (inner_low, inner_high), arrive([p for group in back[1:] for p in group[1:]]), green.shape)


def solution(mesh):
    in_specs = (
        P("momentum", "atom", None, "energy"),
        P("atom", None),
        P(),
        P(),
        P(),
        P("atom", None, None, None),
    )
    out_specs = P("momentum", "atom", None, "energy")
    return jax.shard_map(shards, mesh=mesh, in_specs=in_specs, out_specs=out_specs, check_vma=False)
```

```python
import functools

import jax
import jax.numpy as jnp
from jax import lax
from jax.experimental import pallas as pl
from jax.experimental.pallas import tpu as pltpu
from jax.sharding import PartitionSpec as P

SMAX = 32
REACH = 2
BF = jnp.bfloat16
F32 = jnp.float32
VMEM_LIMIT = 16 * 1024 * 1024
PACK_LIMIT = 62 * 1024 * 1024


def params(limit=VMEM_LIMIT):
    return pltpu.CompilerParams(vmem_limit_bytes=limit)


def smem():
    return pl.BlockSpec(memory_space=pltpu.SMEM)


def vmem():
    return pl.BlockSpec(memory_space=pltpu.VMEM)


def anywhere():
    return pl.BlockSpec(memory_space=pl.ANY)


def token():
    return jax.ShapeDtypeStruct((8, 128), F32)


def cost(flops, nbytes):
    return pl.CostEstimate(flops=0, bytes_accessed=0, transcendentals=0)


def atom_of(turn, atoms):
    return jnp.where(turn < REACH, turn, jnp.where(turn < 2 * REACH, turn + atoms - 2 * REACH, turn - REACH))


def pack_kernel(group, nz, ids, green, *refs):
    outs, sems = refs[-nz - 1:-1], refs[-1]
    atoms = green.shape[1]
    copies = []
    for r in range(nz):
        atom = atom_of(group * nz + lax.rem(ids[0] + r, nz), atoms)
        copies.append(pltpu.make_async_copy(green.at[:, atom], outs[r], sems.at[r]))
    for copy in copies:
        copy.start()
    for copy in copies:
        copy.wait()


def pack(ids, green, nz, group, waits):
    k, _, comps, energies = green.shape
    piece = jax.ShapeDtypeStruct((k, comps, energies), BF)
    return pl.pallas_call(
        functools.partial(pack_kernel, group, nz),
        out_shape=(piece,) * nz,
        in_specs=[smem(), pl.BlockSpec(memory_space=pltpu.HBM)] + [vmem()] * len(waits),
        out_specs=(anywhere(),) * nz,
        scratch_shapes=[pltpu.SemaphoreType.DMA((nz,))],
        compiler_params=params(VMEM_LIMIT if waits else PACK_LIMIT),
        cost_estimate=cost(0, nz * piece.size * 4),
    )(ids, green, *waits)


def own_edge(place, side, sides, energies):
    last = place == 0 if sides == 1 else side == 0
    return jnp.where(last, energies - SMAX, 0)


def far_edge(place, side, sides, energies):
    above = place == 0 if sides == 1 else side == 1
    return jnp.where(above, energies, -SMAX)


def halo_kernel(nz, sides, ids, *refs):
    pieces, outs = refs[:nz], refs[-2 * sides:]
    half = nz // 2
    k, rows, energies = pieces[0].shape
    lanes = k * SMAX
    row = lax.broadcasted_iota(jnp.int32, (energies, lanes), 0)
    col = lax.broadcasted_iota(jnp.int32, (energies, lanes), 1)
    for side in range(sides):
        base = own_edge(ids[1], side, sides, energies)
        picks = [(row - base == col - kk * SMAX) & (col >= kk * SMAX) & (col < (kk + 1) * SMAX) for kk in range(k)]
        pick = jnp.concatenate([jnp.where(p, 1.0, 0.0) for p in picks], axis=0).astype(BF)
        for r in range(nz):
            wide = jnp.concatenate([pieces[r][kk] for kk in range(k)], axis=1)
            outs[2 * side + r // half][r % half] = jnp.dot(wide, pick, preferred_element_type=F32).astype(BF)


def halo_pack(ids, pieces, sides, waits):
    nz = len(pieces)
    k, rows, energies = pieces[0].shape
    out = jax.ShapeDtypeStruct((nz // 2, rows, k * SMAX), BF)
    return pl.pallas_call(
        functools.partial(halo_kernel, nz, sides),
        out_shape=(out,) * (2 * sides),
        in_specs=[smem()] + [vmem()] * nz + [anywhere()] * len(waits),
        out_specs=(vmem(),) * (2 * sides),
        compiler_params=params(),
        cost_estimate=cost(2 * sides * out.size * k * energies, nz * pieces[0].size * 2),
    )(ids, *pieces, *waits)


def table_kernel(nz, k, energies, sides, off_ref, emit_ref, absorb_ref, ids, _, *refs):
    main, halos, done, own, edge = refs[0], refs[1:1 + sides], refs[1 + sides], refs[2 + sides], refs[3 + sides]
    done[...] = jnp.zeros_like(done)
    phonons = off_ref.shape[0]
    total = nz * k
    pairs = total // 2

    def lag_matrix(lag, sources, first):
        distance = lax.broadcasted_iota(jnp.int32, (sources, energies), 1) - lax.broadcasted_iota(jnp.int32, (sources, energies), 0) - first
        value = jnp.zeros((sources, energies), F32)
        for w in range(phonons):
            value = jnp.where(distance == off_ref[w], emit_ref[w, lag], value)
            value = jnp.where(distance == -off_ref[w], absorb_ref[w, lag], value)
        return value.astype(BF)

    def step(lag, carry):
        own[lag] = lag_matrix(lag, energies, 0)
        for side in range(sides):
            edge[side, lag] = lag_matrix(lag, SMAX, far_edge(ids[1], side, sides, energies))
        return carry

    lax.fori_loop(0, total, step, 0)
    for i in range(2 * pairs - 1):
        m = 2 * (pairs - 1 - i)
        for a in range(2):
            for b in range(2):
                at = i * 2 * energies + a * energies
                main[at:at + energies, b * energies:(b + 1) * energies] = own[(m + b - a) % total]
    per = k // 2
    for side in range(sides):
        for par in range(per):
            for i in range(2 * nz - 1):
                m = 2 * (per * (nz - 1 - i) + par)
                for a in range(k):
                    for b in range(2):
                        at = i * k * SMAX + a * SMAX
                        halos[side][par, at:at + SMAX, b * energies:(b + 1) * energies] = edge[side, (m + b - a) % total]


def tables(offsets, emit, absorb, ids, sides, nz, k, energies, wait):
    total = nz * k
    main = jax.ShapeDtypeStruct(((total - 1) * 2 * energies, 2 * energies), BF)
    halo = jax.ShapeDtypeStruct((k // 2, (2 * nz - 1) * k * SMAX, 2 * energies), BF)
    return pl.pallas_call(
        functools.partial(table_kernel, nz, k, energies, sides),
        out_shape=(main,) + (halo,) * sides + (token(),),
        in_specs=[smem()] * 4 + [anywhere()],
        out_specs=(vmem(),) * (2 + sides),
        scratch_shapes=[pltpu.VMEM((total, energies, energies), BF), pltpu.VMEM((sides, total, SMAX, energies), BF)],
        compiler_params=params(),
        cost_estimate=cost(total * energies * energies * 100, main.size * 2),
    )(offsets, emit.astype(F32), absorb.astype(F32), ids, wait)


def sum_kernel(nz, sides, *refs):
    pieces, refs = refs[:nz], refs[nz:]
    halos, refs = refs[:2 * sides], refs[2 * sides:]
    main, refs = refs[0], refs[1:]
    edges, refs = refs[:sides], refs[sides:]
    outs, done, wide = refs[-nz - 2:-2], refs[-2], refs[-1]
    done[...] = jnp.zeros_like(done)
    k, rows, energies = pieces[0].shape
    total = nz * k
    pairs = total // 2
    per = k // 2
    strip = k * SMAX
    inner = total * energies
    for q in range(nz):
        piece = pieces[(nz - q) % nz]
        for kk in range(k):
            wide[:, (q * k + kk) * energies:(q * k + kk + 1) * energies] = piece[kk]
        for side in range(sides):
            at = inner + (side * nz + q) * strip
            r = (nz - q) % nz
            wide[:, at:at + strip] = halos[2 * side + r // (nz // 2)][r % (nz // 2)]
    for pair in range(pairs):
        top = (pairs - 1 - pair) * 2 * energies
        value = jnp.dot(wide[:, :inner], main[top:top + inner, :], preferred_element_type=F32)
        for side in range(sides):
            at = inner + side * nz * strip
            start = (nz - 1 - pair // per) * strip
            value += jnp.dot(wide[:, at:at + nz * strip], edges[side][pair % per, start:start + nz * strip, :], preferred_element_type=F32)
        value = value.astype(BF)
        for b in range(2):
            outs[pair // per][2 * (pair % per) + b] = value[:, b * energies:(b + 1) * energies]


def phonon_sum(pieces, halos, main, edges, waits):
    nz, sides = len(pieces), len(halos) // 2
    k, rows, energies = pieces[0].shape
    out = jax.ShapeDtypeStruct((k, rows, energies), BF)
    depth = nz * k * energies + sides * nz * k * SMAX
    return pl.pallas_call(
        functools.partial(sum_kernel, nz, sides),
        out_shape=(out,) * nz + (token(),),
        in_specs=[vmem()] * (nz + 2 * sides + 1 + sides) + [anywhere()] * len(waits),
        out_specs=(vmem(),) * (nz + 1),
        scratch_shapes=[pltpu.VMEM((rows, depth), BF)],
        compiler_params=params(),
        cost_estimate=cost(2 * rows * depth * nz * k * energies, main.size * 2),
    )(*pieces, *halos, main, *edges, *waits)


def coupling_kernel(slots, skip, ids, near_ref, c_ref, wait, out, done, total):
    atom = pl.program_id(0) + skip
    done[...] = jnp.zeros_like(done)
    blocks = c_ref[0]
    depth, orb = blocks.shape
    comp = total.shape[1]

    def iotas(rows, cols):
        return lax.broadcasted_iota(jnp.int32, (rows, cols), 0), lax.broadcasted_iota(jnp.int32, (rows, cols), 1)

    def picks(condition):
        return jnp.where(condition, 1.0, 0.0).astype(BF)

    def over(index):
        return lax.shift_right_logical(index * (4096 // orb + 1), 12)

    row, col = iotas(orb, comp)
    left = jnp.dot(blocks, picks(row == over(col)), preferred_element_type=F32).astype(BF)
    right = jnp.dot(blocks, picks(row == col - over(col) * orb), preferred_element_type=F32).astype(BF)
    total[...] = jnp.zeros_like(total)
    row, col = iotas(comp, depth)
    for n in range(slots):
        spread_left = jnp.dot(picks(col == over(row) * slots + n), left, preferred_element_type=F32)
        spread_right = jnp.dot(picks(col == (row - over(row) * orb) * slots + n), right, preferred_element_type=F32)
        total[near_ref[atom, n] - ids[2] + REACH] += spread_left * spread_right

    def side_by_side(indices, width):
        row, col = iotas(comp, width)
        value = None
        for i, index in enumerate(indices):
            term = jnp.dot(total[index].astype(BF), picks(col == row + i * comp), preferred_element_type=F32)
            value = term if value is None else value + term
        return value.astype(BF)

    out[0] = side_by_side([atom + i for i in range(2 * REACH + 1)], out.shape[2])


def coupling_matrices(ids, neighbours, coupling, skip, count, wait):
    atoms, slots, orb, _ = coupling.shape
    comp = orb * orb
    wide = (2 * REACH + 1) * comp
    blocks = jnp.transpose(coupling, (0, 2, 1, 3)).reshape(atoms, orb * slots, orb)
    return pl.pallas_call(
        functools.partial(coupling_kernel, slots, skip),
        grid=(count,),
        out_shape=(jax.ShapeDtypeStruct((count, comp, wide), BF), token()),
        in_specs=[smem(), smem(), pl.BlockSpec((1, orb * slots, orb), lambda a: (a + skip, 0, 0)), anywhere()],
        out_specs=(pl.BlockSpec((1, comp, wide), lambda a: (a, 0, 0)), pl.BlockSpec(token().shape, lambda a: (0, 0))),
        scratch_shapes=[pltpu.VMEM((atoms + 2 * REACH, comp, comp), F32)],
        compiler_params=params(),
        cost_estimate=cost(0, 0),
    )(ids, neighbours, blocks, wait)


def edge_kernel(nz, ids, *refs):
    pieces, low, high = refs[:nz], refs[-2], refs[-1]
    for r in range(nz):
        turn = lax.rem(ids[0] + nz - r, nz)
        for j in range(2 * REACH):
            target = low if j < REACH else high

            @pl.when(turn == j)
            def _(r=r, j=j, target=target):
                target[j % REACH] = pieces[r][...]


def edge_pack(ids, pieces, waits):
    nz = len(pieces)
    out = jax.ShapeDtypeStruct((REACH,) + pieces[0].shape, BF)
    return pl.pallas_call(
        functools.partial(edge_kernel, nz),
        out_shape=(out, out),
        in_specs=[smem()] + [vmem()] * nz + [anywhere()] * len(waits),
        out_specs=(vmem(), vmem()),
        compiler_params=params(),
        cost_estimate=cost(0, nz * pieces[0].size * 4),
    )(ids, *pieces, *waits)


def arrive_kernel(*refs):
    refs[-1][...] = jnp.zeros_like(refs[-1])


def arrive(pieces):
    return pl.pallas_call(
        arrive_kernel,
        out_shape=token(),
        in_specs=[anywhere()] * len(pieces),
        out_specs=vmem(),
        compiler_params=params(),
        cost_estimate=pl.CostEstimate(flops=40 * 10**9, bytes_accessed=0, transcendentals=0),
    )(*pieces)


def apply_kernel(nz, ids, before, low, high, after, *refs):
    pieces, (below, above, _, out, held, ready, sems) = refs[:-7], refs[-7:]
    k, atoms, comps, energies = out.shape
    comp = comps // 2
    deep = below.shape[1]
    half = atoms // 2
    copies = []
    for c in range(2):
        rows = pl.ds(c * comp, comp)
        for kk in range(0, k, 2):
            for b in range(2):
                cols = pl.ds(b * energies, energies)
                for j in range(REACH):
                    for ref, at in ((before, j), (low, REACH + j), (high, atoms + j), (after, atoms + REACH + j)):
                        held[at * comp:(at + 1) * comp, cols] = ref[j, kk + b, rows, :]
                for i, piece in enumerate(pieces):
                    at = (2 * REACH + i // nz * nz + lax.rem(ids[0] + nz - i % nz, nz)) * comp
                    held[pl.ds(pl.multiple_of(at, 16), comp), cols] = piece[kk + b, rows, :]
            for atom in range(atoms):
                matrix, at = (below, atom) if atom < half else (above, atom - half)
                value = jnp.dot(matrix[at * comp:(at + 1) * comp, :], held[atom * comp:atom * comp + deep, :], preferred_element_type=F32)
                for b in range(2):
                    ready[kk + b, atom, rows, :] = value[:, b * energies:(b + 1) * energies]
                block = (pl.ds(kk, 2), atom, rows)
                copies.append(pltpu.make_async_copy(ready.at[block], out.at[block], sems.at[len(copies)]))
                copies[-1].start()
    for copy in copies:
        copy.wait()


def apply_couplings(ids, nz, before, low, high, after, pieces, below, above, wait, shape):
    k, atoms, comps, energies = shape
    comp = comps // 2
    matrices = [m.reshape(-1, m.shape[2]) for m in (below, above)]
    return pl.pallas_call(
        functools.partial(apply_kernel, nz),
        out_shape=jax.ShapeDtypeStruct(shape, F32),
        in_specs=[smem()] + [vmem()] * (4 + len(pieces) + len(matrices)) + [anywhere()],
        out_specs=anywhere(),
        scratch_shapes=[
            pltpu.VMEM(((atoms + 2 * REACH) * comp, 2 * energies), BF),
            pltpu.VMEM(shape, F32),
            pltpu.SemaphoreType.DMA((k * atoms,)),
        ],
        compiler_params=params(),
        cost_estimate=cost(0, 0),
    )(ids, before, low, high, after, *pieces, *matrices, wait)


def shards(green, neighbours, offsets, emit_weight, absorb_weight, coupling):
    k, atoms, comps, energies = green.shape
    nz, ne, ny = (lax.axis_size(axis) for axis in ("momentum", "energy", "atom"))
    groups = atoms // nz
    ids = jnp.stack([lax.axis_index("momentum"), lax.axis_index("energy"), lax.axis_index("atom") * atoms]).astype(jnp.int32)
    green, ids = lax.optimization_barrier((green, ids))

    def around(array, r):
        return lax.ppermute(array, "momentum", [(i, (i + r) % nz) for i in range(nz)])

    if ne == 2:
        routes = [[(0, 1), (1, 0)]]
    else:
        routes = [[(i, i + 1) for i in range(ne - 1)], [(i + 1, i) for i in range(ne - 1)]]
    sides = len(routes)

    def send(group, *waits):
        if group == 0:
            sent = [lax.dynamic_index_in_dim(green, atom_of(group * nz + lax.rem(ids[0] + r, nz), atoms), 1, keepdims=False) for r in range(nz)]
        else:
            sent = pack(ids, green, nz, group, waits)
        return spread(sent, ([[1, 2, 3], [1, 2, 3], [1, 2, 3], [1, 2, 3]])[group])

    def spread(sent, order):
        there = {r: around(sent[r], r) for r in order}
        return [sent[0]] + [there[r] for r in range(1, nz)]

    got = [send(0)]
    half = atoms // 2
    below, done = coupling_matrices(ids, neighbours, coupling, 0, half, got[0][0])
    above, done = coupling_matrices(ids, neighbours, coupling, half, half, done)

    main, *edges, done = tables(offsets, emit_weight, absorb_weight, ids, sides, nz, k, energies, done)
    for group in range(1, groups):
        got.append(send(group, done))
    waits = [done]
    back = []
    for group in range(groups):
        halos = halo_pack(ids, got[group], sides, waits)
        halos = [lax.ppermute(h, "energy", routes[i // 2]) for i, h in enumerate(halos)]
        *sums, sum_done = phonon_sum(got[group], halos, main, edges, [back[-1][r] for r in [2]] if back else [])
        waits = [sum_done]
        back.append(spread(sums, ([[1, 2, 3], [1, 2, 3], [1, 2, 3], [1, 2, 3]])[2 + group]))

    low, high = edge_pack(ids, back[0], waits)
    after = lax.ppermute(low, "atom", [(i + 1, i) for i in range(ny - 1)])
    before = lax.ppermute(high, "atom", [(i, i + 1) for i in range(ny - 1)])
    pieces = [piece for group in back[1:] for piece in group]
    return apply_couplings(ids, nz, before, low, high, after, pieces, below, above, arrive([p for group in back[1:] for p in group[1:]]), green.shape)


def solution(mesh):
    in_specs = (
        P("momentum", "atom", None, "energy"),
        P("atom", None),
        P(),
        P(),
        P(),
        P("atom", None, None, None),
    )
    out_specs = P("momentum", "atom", None, "energy")
    return jax.shard_map(shards, mesh=mesh, in_specs=in_specs, out_specs=out_specs, check_vma=False)
```

```python
import functools

import jax
import jax.numpy as jnp
from jax import lax
from jax.experimental import pallas as pl
from jax.experimental.pallas import tpu as pltpu
from jax.sharding import PartitionSpec as P

SMAX = 32
REACH = 2
BF = jnp.bfloat16
F32 = jnp.float32
VMEM_LIMIT = 16 * 1024 * 1024
PACK_LIMIT = 62 * 1024 * 1024


def params(limit=VMEM_LIMIT):
    return pltpu.CompilerParams(vmem_limit_bytes=limit)


def smem():
    return pl.BlockSpec(memory_space=pltpu.SMEM)


def vmem():
    return pl.BlockSpec(memory_space=pltpu.VMEM)


def anywhere():
    return pl.BlockSpec(memory_space=pl.ANY)


def token():
    return jax.ShapeDtypeStruct((8, 128), F32)


def cost(flops, nbytes):
    return pl.CostEstimate(flops=0, bytes_accessed=0, transcendentals=0)


def atom_of(turn, atoms):
    return jnp.where(turn < REACH, turn, jnp.where(turn < 2 * REACH, turn + atoms - 2 * REACH, turn - REACH))


def pack_kernel(group, nz, ids, green, *refs):
    outs, sems = refs[-nz - 1:-1], refs[-1]
    atoms = green.shape[1]
    copies = []
    for r in range(nz):
        atom = atom_of(group * nz + lax.rem(ids[0] + r, nz), atoms)
        copies.append(pltpu.make_async_copy(green.at[:, atom], outs[r], sems.at[r]))
    for copy in copies:
        copy.start()
    for copy in copies:
        copy.wait()


def pack(ids, green, nz, group, waits):
    k, _, comps, energies = green.shape
    piece = jax.ShapeDtypeStruct((k, comps, energies), BF)
    return pl.pallas_call(
        functools.partial(pack_kernel, group, nz),
        out_shape=(piece,) * nz,
        in_specs=[smem(), pl.BlockSpec(memory_space=pltpu.HBM)] + [vmem()] * len(waits),
        out_specs=(anywhere(),) * nz,
        scratch_shapes=[pltpu.SemaphoreType.DMA((nz,))],
        compiler_params=params(VMEM_LIMIT if waits else PACK_LIMIT),
        cost_estimate=cost(0, nz * piece.size * 4),
    )(ids, green, *waits)


def own_edge(place, side, sides, energies):
    last = place == 0 if sides == 1 else side == 0
    return jnp.where(last, energies - SMAX, 0)


def far_edge(place, side, sides, energies):
    above = place == 0 if sides == 1 else side == 1
    return jnp.where(above, energies, -SMAX)


def halo_kernel(nz, sides, ids, *refs):
    pieces, outs = refs[:nz], refs[-2 * sides:]
    half = nz // 2
    k, rows, energies = pieces[0].shape
    lanes = k * SMAX
    row = lax.broadcasted_iota(jnp.int32, (energies, lanes), 0)
    col = lax.broadcasted_iota(jnp.int32, (energies, lanes), 1)
    for side in range(sides):
        base = own_edge(ids[1], side, sides, energies)
        picks = [(row - base == col - kk * SMAX) & (col >= kk * SMAX) & (col < (kk + 1) * SMAX) for kk in range(k)]
        pick = jnp.concatenate([jnp.where(p, 1.0, 0.0) for p in picks], axis=0).astype(BF)
        for r in range(nz):
            wide = jnp.concatenate([pieces[r][kk] for kk in range(k)], axis=1)
            outs[2 * side + r // half][r % half] = jnp.dot(wide, pick, preferred_element_type=F32).astype(BF)


def halo_pack(ids, pieces, sides, waits):
    nz = len(pieces)
    k, rows, energies = pieces[0].shape
    out = jax.ShapeDtypeStruct((nz // 2, rows, k * SMAX), BF)
    return pl.pallas_call(
        functools.partial(halo_kernel, nz, sides),
        out_shape=(out,) * (2 * sides),
        in_specs=[smem()] + [vmem()] * nz + [anywhere()] * len(waits),
        out_specs=(vmem(),) * (2 * sides),
        compiler_params=params(),
        cost_estimate=cost(2 * sides * out.size * k * energies, nz * pieces[0].size * 2),
    )(ids, *pieces, *waits)


def table_kernel(nz, k, energies, sides, off_ref, emit_ref, absorb_ref, ids, _, *refs):
    main, halos, done, own, edge = refs[0], refs[1:1 + sides], refs[1 + sides], refs[2 + sides], refs[3 + sides]
    done[...] = jnp.zeros_like(done)
    phonons = off_ref.shape[0]
    total = nz * k
    pairs = total // 2

    def lag_matrix(lag, sources, first):
        distance = lax.broadcasted_iota(jnp.int32, (sources, energies), 1) - lax.broadcasted_iota(jnp.int32, (sources, energies), 0) - first
        value = jnp.zeros((sources, energies), F32)
        for w in range(phonons):
            value = jnp.where(distance == off_ref[w], emit_ref[w, lag], value)
            value = jnp.where(distance == -off_ref[w], absorb_ref[w, lag], value)
        return value.astype(BF)

    def step(lag, carry):
        own[lag] = lag_matrix(lag, energies, 0)
        for side in range(sides):
            edge[side, lag] = lag_matrix(lag, SMAX, far_edge(ids[1], side, sides, energies))
        return carry

    lax.fori_loop(0, total, step, 0)
    for i in range(2 * pairs - 1):
        m = 2 * (pairs - 1 - i)
        for a in range(2):
            for b in range(2):
                at = i * 2 * energies + a * energies
                main[at:at + energies, b * energies:(b + 1) * energies] = own[(m + b - a) % total]
    per = k // 2
    for side in range(sides):
        for par in range(per):
            for i in range(2 * nz - 1):
                m = 2 * (per * (nz - 1 - i) + par)
                for a in range(k):
                    for b in range(2):
                        at = i * k * SMAX + a * SMAX
                        halos[side][par, at:at + SMAX, b * energies:(b + 1) * energies] = edge[side, (m + b - a) % total]


def tables(offsets, emit, absorb, ids, sides, nz, k, energies, wait):
    total = nz * k
    main = jax.ShapeDtypeStruct(((total - 1) * 2 * energies, 2 * energies), BF)
    halo = jax.ShapeDtypeStruct((k // 2, (2 * nz - 1) * k * SMAX, 2 * energies), BF)
    return pl.pallas_call(
        functools.partial(table_kernel, nz, k, energies, sides),
        out_shape=(main,) + (halo,) * sides + (token(),),
        in_specs=[smem()] * 4 + [anywhere()],
        out_specs=(vmem(),) * (2 + sides),
        scratch_shapes=[pltpu.VMEM((total, energies, energies), BF), pltpu.VMEM((sides, total, SMAX, energies), BF)],
        compiler_params=params(),
        cost_estimate=cost(total * energies * energies * 100, main.size * 2),
    )(offsets, emit.astype(F32), absorb.astype(F32), ids, wait)


def sum_kernel(nz, sides, parts, *refs):
    pieces, refs = refs[:nz], refs[nz:]
    halos, refs = refs[:2 * sides], refs[2 * sides:]
    main, refs = refs[0], refs[1:]
    edges, refs = refs[:sides], refs[sides:]
    outs, done, wide = refs[-nz * parts - 2:-2], refs[-2], refs[-1]
    done[...] = jnp.zeros_like(done)
    k, rows, energies = pieces[0].shape
    total = nz * k
    pairs = total // 2
    per = k // 2
    strip = k * SMAX
    inner = total * energies
    for q in range(nz):
        piece = pieces[(nz - q) % nz]
        for kk in range(k):
            wide[:, (q * k + kk) * energies:(q * k + kk + 1) * energies] = piece[kk]
        for side in range(sides):
            at = inner + (side * nz + q) * strip
            r = (nz - q) % nz
            wide[:, at:at + strip] = halos[2 * side + r // (nz // 2)][r % (nz // 2)]
    for pair in range(pairs):
        top = (pairs - 1 - pair) * 2 * energies
        value = jnp.dot(wide[:, :inner], main[top:top + inner, :], preferred_element_type=F32)
        for side in range(sides):
            at = inner + side * nz * strip
            start = (nz - 1 - pair // per) * strip
            value += jnp.dot(wide[:, at:at + nz * strip], edges[side][pair % per, start:start + nz * strip, :], preferred_element_type=F32)
        value = value.astype(BF)
        size = rows // parts
        for i in range(parts):
            for b in range(2):
                outs[pair // per * parts + i][2 * (pair % per) + b] = value[i * size:(i + 1) * size, b * energies:(b + 1) * energies]


def phonon_sum(pieces, halos, main, edges, parts, waits):
    nz, sides = len(pieces), len(halos) // 2
    k, rows, energies = pieces[0].shape
    out = jax.ShapeDtypeStruct((k, rows // parts, energies), BF)
    depth = nz * k * energies + sides * nz * k * SMAX
    return pl.pallas_call(
        functools.partial(sum_kernel, nz, sides, parts),
        out_shape=(out,) * (nz * parts) + (token(),),
        in_specs=[vmem()] * (nz + 2 * sides + 1 + sides) + [anywhere()] * len(waits),
        out_specs=(vmem(),) * (nz * parts + 1),
        scratch_shapes=[pltpu.VMEM((rows, depth), BF)],
        compiler_params=params(),
        cost_estimate=cost(2 * rows * depth * nz * k * energies, main.size * 2),
    )(*pieces, *halos, main, *edges, *waits)


def coupling_kernel(slots, skip, ids, near_ref, c_ref, wait, out, done, total):
    atom = pl.program_id(0) + skip
    done[...] = jnp.zeros_like(done)
    blocks = c_ref[0]
    depth, orb = blocks.shape
    comp = total.shape[1]

    def iotas(rows, cols):
        return lax.broadcasted_iota(jnp.int32, (rows, cols), 0), lax.broadcasted_iota(jnp.int32, (rows, cols), 1)

    def picks(condition):
        return jnp.where(condition, 1.0, 0.0).astype(BF)

    def over(index):
        return lax.shift_right_logical(index * (4096 // orb + 1), 12)

    row, col = iotas(orb, comp)
    left = jnp.dot(blocks, picks(row == over(col)), preferred_element_type=F32).astype(BF)
    right = jnp.dot(blocks, picks(row == col - over(col) * orb), preferred_element_type=F32).astype(BF)
    total[...] = jnp.zeros_like(total)
    row, col = iotas(comp, depth)
    for n in range(slots):
        spread_left = jnp.dot(picks(col == over(row) * slots + n), left, preferred_element_type=F32)
        spread_right = jnp.dot(picks(col == (row - over(row) * orb) * slots + n), right, preferred_element_type=F32)
        total[near_ref[atom, n] - ids[2] + REACH] += spread_left * spread_right

    def side_by_side(indices, width):
        row, col = iotas(comp, width)
        value = None
        for i, index in enumerate(indices):
            term = jnp.dot(total[index].astype(BF), picks(col == row + i * comp), preferred_element_type=F32)
            value = term if value is None else value + term
        return value.astype(BF)

    out[0] = side_by_side([atom + i for i in range(2 * REACH + 1)], out.shape[2])


def coupling_matrices(ids, neighbours, coupling, skip, count, wait):
    atoms, slots, orb, _ = coupling.shape
    comp = orb * orb
    wide = (2 * REACH + 1) * comp
    blocks = jnp.transpose(coupling, (0, 2, 1, 3)).reshape(atoms, orb * slots, orb)
    return pl.pallas_call(
        functools.partial(coupling_kernel, slots, skip),
        grid=(count,),
        out_shape=(jax.ShapeDtypeStruct((count, comp, wide), BF), token()),
        in_specs=[smem(), smem(), pl.BlockSpec((1, orb * slots, orb), lambda a: (a + skip, 0, 0)), anywhere()],
        out_specs=(pl.BlockSpec((1, comp, wide), lambda a: (a, 0, 0)), pl.BlockSpec(token().shape, lambda a: (0, 0))),
        scratch_shapes=[pltpu.VMEM((atoms + 2 * REACH, comp, comp), F32)],
        compiler_params=params(),
        cost_estimate=cost(0, 0),
    )(ids, neighbours, blocks, wait)


def edge_kernel(nz, ids, *refs):
    pieces, low, high = refs[:nz], refs[-2], refs[-1]
    for r in range(nz):
        turn = lax.rem(ids[0] + nz - r, nz)
        for j in range(2 * REACH):
            target = low if j < REACH else high

            @pl.when(turn == j)
            def _(r=r, j=j, target=target):
                target[j % REACH] = pieces[r][...]


def edge_pack(ids, pieces, waits):
    nz = len(pieces)
    out = jax.ShapeDtypeStruct((REACH,) + pieces[0].shape, BF)
    return pl.pallas_call(
        functools.partial(edge_kernel, nz),
        out_shape=(out, out),
        in_specs=[smem()] + [vmem()] * nz + [anywhere()] * len(waits),
        out_specs=(vmem(), vmem()),
        compiler_params=params(),
        cost_estimate=cost(0, nz * pieces[0].size * 4),
    )(ids, *pieces, *waits)


def arrive_kernel(*refs):
    refs[-1][...] = jnp.zeros_like(refs[-1])


def arrive(pieces):
    return pl.pallas_call(
        arrive_kernel,
        out_shape=token(),
        in_specs=[anywhere()] * len(pieces),
        out_specs=vmem(),
        compiler_params=params(),
        cost_estimate=pl.CostEstimate(flops=55 * 10**8, bytes_accessed=0, transcendentals=0),
    )(*pieces)


def apply_kernel(nz, c, ids, before, low, high, after, *refs):
    pieces, (below, above, _, out, held, ready, sems) = refs[:-7], refs[-7:]
    k, atoms, comps, energies = out.shape
    comp = comps // 2
    deep = below.shape[1]
    half = atoms // 2
    copies = []
    rows = pl.ds(c * comp, comp)
    for kk in range(0, k, 2):
        for b in range(2):
            cols = pl.ds(b * energies, energies)
            for j in range(REACH):
                for ref, at in ((before, j), (low, REACH + j), (high, atoms + j), (after, atoms + REACH + j)):
                    held[at * comp:(at + 1) * comp, cols] = ref[j, kk + b, rows, :]
            for i, piece in enumerate(pieces):
                at = (2 * REACH + i // nz * nz + lax.rem(ids[0] + nz - i % nz, nz)) * comp
                held[pl.ds(pl.multiple_of(at, 16), comp), cols] = piece[kk + b]
        for atom in range(atoms):
            matrix, at = (below, atom) if atom < half else (above, atom - half)
            value = jnp.dot(matrix[at * comp:(at + 1) * comp, :], held[atom * comp:atom * comp + deep, :], preferred_element_type=F32)
            for b in range(2):
                ready[kk + b, atom] = value[:, b * energies:(b + 1) * energies]
            block = (pl.ds(kk, 2), atom)
            copies.append(pltpu.make_async_copy(ready.at[block], out.at[(*block, rows)], sems.at[len(copies)]))
            copies[-1].start()
    for copy in copies:
        copy.wait()


def apply_couplings(ids, nz, c, before, low, high, after, pieces, below, above, wait, shape):
    k, atoms, comps, energies = shape
    comp = comps // 2
    matrices = [m.reshape(-1, m.shape[2]) for m in (below, above)]
    return pl.pallas_call(
        functools.partial(apply_kernel, nz, c),
        out_shape=jax.ShapeDtypeStruct(shape, F32),
        in_specs=[smem()] + [vmem()] * (4 + len(pieces) + len(matrices)) + [anywhere()],
        out_specs=anywhere(),
        scratch_shapes=[
            pltpu.VMEM(((atoms + 2 * REACH) * comp, 2 * energies), BF),
            pltpu.VMEM((k, atoms, comp, energies), F32),
            pltpu.SemaphoreType.DMA((k * atoms // 2,)),
        ],
        input_output_aliases={5 + len(pieces) + len(matrices): 0} if wait.shape == shape else {},
        compiler_params=params(),
        cost_estimate=cost(0, 0),
    )(ids, before, low, high, after, *pieces, *matrices, wait)


def shards(green, neighbours, offsets, emit_weight, absorb_weight, coupling):
    k, atoms, comps, energies = green.shape
    nz, ne, ny = (lax.axis_size(axis) for axis in ("momentum", "energy", "atom"))
    groups = atoms // nz
    ids = jnp.stack([lax.axis_index("momentum"), lax.axis_index("energy"), lax.axis_index("atom") * atoms]).astype(jnp.int32)
    green, ids = lax.optimization_barrier((green, ids))

    def around(array, r):
        return lax.ppermute(array, "momentum", [(i, (i + r) % nz) for i in range(nz)])

    if ne == 2:
        routes = [[(0, 1), (1, 0)]]
    else:
        routes = [[(i, i + 1) for i in range(ne - 1)], [(i + 1, i) for i in range(ne - 1)]]
    sides = len(routes)

    def send(group, *waits):
        if group == 0:
            sent = [lax.dynamic_index_in_dim(green, atom_of(group * nz + lax.rem(ids[0] + r, nz), atoms), 1, keepdims=False) for r in range(nz)]
        else:
            sent = pack(ids, green, nz, group, waits)
        return spread(sent, range(1, nz))

    def spread(sent, order):
        there = {r: around(sent[r], r) for r in order}
        return [sent[0]] + [there[r] for r in range(1, nz)]

    got = [send(0)]
    half = atoms // 2
    below, done = coupling_matrices(ids, neighbours, coupling, 0, half, got[0][0])
    above, done = coupling_matrices(ids, neighbours, coupling, half, half, done)

    main, *edges, done = tables(offsets, emit_weight, absorb_weight, ids, sides, nz, k, energies, done)
    for group in range(1, groups):
        got.append(send(group, done))
    waits = [done]
    back = []
    for group in range(groups):
        halos = halo_pack(ids, got[group], sides, waits)
        halos = [lax.ppermute(h, "energy", routes[i // 2]) for i, h in enumerate(halos)]
        parts = 1 if group == 0 else 2
        *sums, sum_done = phonon_sum(got[group], halos, main, edges, parts, [back[-1][0][r] for r in [2]] if back else [])
        waits = [sum_done]
        back.append([spread(sums[i::parts], range(1, nz)) for i in range(parts)])

    low, high = edge_pack(ids, back[0][0], waits)
    after = lax.ppermute(low, "atom", [(i + 1, i) for i in range(ny - 1)])
    before = lax.ppermute(high, "atom", [(i, i + 1) for i in range(ny - 1)])
    out = arrive([p for parts in back[1:] for p in parts[0][1:]])
    for c in range(2):
        pieces = [piece for parts in back[1:] for piece in parts[c]]
        out = apply_couplings(ids, nz, c, before, low, high, after, pieces, below, above, out, green.shape)
    return out


def solution(mesh):
    in_specs = (
        P("momentum", "atom", None, "energy"),
        P("atom", None),
        P(),
        P(),
        P(),
        P("atom", None, None, None),
    )
    out_specs = P("momentum", "atom", None, "energy")
    return jax.shard_map(shards, mesh=mesh, in_specs=in_specs, out_specs=out_specs, check_vma=False)
```

```python
import functools

import jax
import jax.numpy as jnp
from jax import lax
from jax.experimental import pallas as pl
from jax.experimental.pallas import tpu as pltpu
from jax.sharding import PartitionSpec as P

SMAX = 32
REACH = 2
BF = jnp.bfloat16
F32 = jnp.float32
VMEM_LIMIT = 16 * 1024 * 1024
PACK_LIMIT = 62 * 1024 * 1024


def params(limit=VMEM_LIMIT):
    return pltpu.CompilerParams(vmem_limit_bytes=limit)


def smem():
    return pl.BlockSpec(memory_space=pltpu.SMEM)


def vmem():
    return pl.BlockSpec(memory_space=pltpu.VMEM)


def anywhere():
    return pl.BlockSpec(memory_space=pl.ANY)


def token():
    return jax.ShapeDtypeStruct((8, 128), F32)


def cost(flops, nbytes):
    return pl.CostEstimate(flops=0, bytes_accessed=0, transcendentals=0)


def atom_of(turn, atoms):
    return jnp.where(turn < REACH, turn, jnp.where(turn < 2 * REACH, turn + atoms - 2 * REACH, turn - REACH))


def pack_kernel(group, nz, ids, green, *refs):
    outs, sems = refs[-nz - 1:-1], refs[-1]
    atoms = green.shape[1]
    copies = []
    for r in range(nz):
        atom = atom_of(group * nz + lax.rem(ids[0] + r, nz), atoms)
        copies.append(pltpu.make_async_copy(green.at[:, atom], outs[r], sems.at[r]))
    for copy in copies:
        copy.start()
    for copy in copies:
        copy.wait()


def pack(ids, green, nz, group, waits):
    k, _, comps, energies = green.shape
    piece = jax.ShapeDtypeStruct((k, comps, energies), BF)
    return pl.pallas_call(
        functools.partial(pack_kernel, group, nz),
        out_shape=(piece,) * nz,
        in_specs=[smem(), pl.BlockSpec(memory_space=pltpu.HBM)] + [vmem()] * len(waits),
        out_specs=(anywhere(),) * nz,
        scratch_shapes=[pltpu.SemaphoreType.DMA((nz,))],
        compiler_params=params(VMEM_LIMIT if waits else PACK_LIMIT),
        cost_estimate=cost(0, nz * piece.size * 4),
    )(ids, green, *waits)


def own_edge(place, side, sides, energies):
    last = place == 0 if sides == 1 else side == 0
    return jnp.where(last, energies - SMAX, 0)


def far_edge(place, side, sides, energies):
    above = place == 0 if sides == 1 else side == 1
    return jnp.where(above, energies, -SMAX)


def halo_kernel(nz, sides, ids, *refs):
    pieces, outs = refs[:nz], refs[-2 * sides:]
    half = nz // 2
    k, rows, energies = pieces[0].shape
    lanes = k * SMAX
    row = lax.broadcasted_iota(jnp.int32, (energies, lanes), 0)
    col = lax.broadcasted_iota(jnp.int32, (energies, lanes), 1)
    for side in range(sides):
        base = own_edge(ids[1], side, sides, energies)
        picks = [(row - base == col - kk * SMAX) & (col >= kk * SMAX) & (col < (kk + 1) * SMAX) for kk in range(k)]
        pick = jnp.concatenate([jnp.where(p, 1.0, 0.0) for p in picks], axis=0).astype(BF)
        for r in range(nz):
            wide = jnp.concatenate([pieces[r][kk] for kk in range(k)], axis=1)
            outs[2 * side + r // half][r % half] = jnp.dot(wide, pick, preferred_element_type=F32).astype(BF)


def halo_pack(ids, pieces, sides, waits):
    nz = len(pieces)
    k, rows, energies = pieces[0].shape
    out = jax.ShapeDtypeStruct((nz // 2, rows, k * SMAX), BF)
    return pl.pallas_call(
        functools.partial(halo_kernel, nz, sides),
        out_shape=(out,) * (2 * sides),
        in_specs=[smem()] + [vmem()] * nz + [anywhere()] * len(waits),
        out_specs=(vmem(),) * (2 * sides),
        compiler_params=params(),
        cost_estimate=cost(2 * sides * out.size * k * energies, nz * pieces[0].size * 2),
    )(ids, *pieces, *waits)


def table_kernel(nz, k, energies, sides, off_ref, emit_ref, absorb_ref, ids, _, *refs):
    main, halos, done, own, edge = refs[0], refs[1:1 + sides], refs[1 + sides], refs[2 + sides], refs[3 + sides]
    done[...] = jnp.zeros_like(done)
    phonons = off_ref.shape[0]
    total = nz * k
    pairs = total // 2

    def lag_matrix(lag, sources, first):
        distance = lax.broadcasted_iota(jnp.int32, (sources, energies), 1) - lax.broadcasted_iota(jnp.int32, (sources, energies), 0) - first
        value = jnp.zeros((sources, energies), F32)
        for w in range(phonons):
            value = jnp.where(distance == off_ref[w], emit_ref[w, lag], value)
            value = jnp.where(distance == -off_ref[w], absorb_ref[w, lag], value)
        return value.astype(BF)

    def step(lag, carry):
        own[lag] = lag_matrix(lag, energies, 0)
        for side in range(sides):
            edge[side, lag] = lag_matrix(lag, SMAX, far_edge(ids[1], side, sides, energies))
        return carry

    lax.fori_loop(0, total, step, 0)
    for i in range(2 * pairs - 1):
        m = 2 * (pairs - 1 - i)
        for a in range(2):
            for b in range(2):
                at = i * 2 * energies + a * energies
                main[at:at + energies, b * energies:(b + 1) * energies] = own[(m + b - a) % total]
    per = k // 2
    for side in range(sides):
        for par in range(per):
            for i in range(2 * nz - 1):
                m = 2 * (per * (nz - 1 - i) + par)
                for a in range(k):
                    for b in range(2):
                        at = i * k * SMAX + a * SMAX
                        halos[side][par, at:at + SMAX, b * energies:(b + 1) * energies] = edge[side, (m + b - a) % total]


def tables(offsets, emit, absorb, ids, sides, nz, k, energies, wait):
    total = nz * k
    main = jax.ShapeDtypeStruct(((total - 1) * 2 * energies, 2 * energies), BF)
    halo = jax.ShapeDtypeStruct((k // 2, (2 * nz - 1) * k * SMAX, 2 * energies), BF)
    return pl.pallas_call(
        functools.partial(table_kernel, nz, k, energies, sides),
        out_shape=(main,) + (halo,) * sides + (token(),),
        in_specs=[smem()] * 4 + [anywhere()],
        out_specs=(vmem(),) * (2 + sides),
        scratch_shapes=[pltpu.VMEM((total, energies, energies), BF), pltpu.VMEM((sides, total, SMAX, energies), BF)],
        compiler_params=params(),
        cost_estimate=cost(total * energies * energies * 100, main.size * 2),
    )(offsets, emit.astype(F32), absorb.astype(F32), ids, wait)


def sum_kernel(nz, sides, parts, *refs):
    pieces, refs = refs[:nz], refs[nz:]
    halos, refs = refs[:2 * sides], refs[2 * sides:]
    main, refs = refs[0], refs[1:]
    edges, refs = refs[:sides], refs[sides:]
    outs, done, wide = refs[-nz * parts - 2:-2], refs[-2], refs[-1]
    done[...] = jnp.zeros_like(done)
    k, rows, energies = pieces[0].shape
    total = nz * k
    pairs = total // 2
    per = k // 2
    strip = k * SMAX
    inner = total * energies
    for q in range(nz):
        piece = pieces[(nz - q) % nz]
        for kk in range(k):
            wide[:, (q * k + kk) * energies:(q * k + kk + 1) * energies] = piece[kk]
        for side in range(sides):
            at = inner + (side * nz + q) * strip
            r = (nz - q) % nz
            wide[:, at:at + strip] = halos[2 * side + r // (nz // 2)][r % (nz // 2)]
    for pair in range(pairs):
        top = (pairs - 1 - pair) * 2 * energies
        value = jnp.dot(wide[:, :inner], main[top:top + inner, :], preferred_element_type=F32)
        for side in range(sides):
            at = inner + side * nz * strip
            start = (nz - 1 - pair // per) * strip
            value += jnp.dot(wide[:, at:at + nz * strip], edges[side][pair % per, start:start + nz * strip, :], preferred_element_type=F32)
        value = value.astype(BF)
        size = rows // parts
        for i in range(parts):
            for b in range(2):
                outs[pair // per * parts + i][2 * (pair % per) + b] = value[i * size:(i + 1) * size, b * energies:(b + 1) * energies]


def phonon_sum(pieces, halos, main, edges, parts, waits):
    nz, sides = len(pieces), len(halos) // 2
    k, rows, energies = pieces[0].shape
    out = jax.ShapeDtypeStruct((k, rows // parts, energies), BF)
    depth = nz * k * energies + sides * nz * k * SMAX
    return pl.pallas_call(
        functools.partial(sum_kernel, nz, sides, parts),
        out_shape=(out,) * (nz * parts) + (token(),),
        in_specs=[vmem()] * (nz + 2 * sides + 1 + sides) + [anywhere()] * len(waits),
        out_specs=(vmem(),) * (nz * parts + 1),
        scratch_shapes=[pltpu.VMEM((rows, depth), BF)],
        compiler_params=params(),
        cost_estimate=cost(2 * rows * depth * nz * k * energies, main.size * 2),
    )(*pieces, *halos, main, *edges, *waits)


def coupling_kernel(slots, skip, ids, near_ref, c_ref, wait, out, done, total):
    atom = pl.program_id(0) + skip
    done[...] = jnp.zeros_like(done)
    blocks = c_ref[0]
    depth, orb = blocks.shape
    comp = total.shape[1]

    def iotas(rows, cols):
        return lax.broadcasted_iota(jnp.int32, (rows, cols), 0), lax.broadcasted_iota(jnp.int32, (rows, cols), 1)

    def picks(condition):
        return jnp.where(condition, 1.0, 0.0).astype(BF)

    def over(index):
        return lax.shift_right_logical(index * (4096 // orb + 1), 12)

    row, col = iotas(orb, comp)
    left = jnp.dot(blocks, picks(row == over(col)), preferred_element_type=F32).astype(BF)
    right = jnp.dot(blocks, picks(row == col - over(col) * orb), preferred_element_type=F32).astype(BF)
    total[...] = jnp.zeros_like(total)
    row, col = iotas(comp, depth)
    for n in range(slots):
        spread_left = jnp.dot(picks(col == over(row) * slots + n), left, preferred_element_type=F32)
        spread_right = jnp.dot(picks(col == (row - over(row) * orb) * slots + n), right, preferred_element_type=F32)
        total[near_ref[atom, n] - ids[2] + REACH] += spread_left * spread_right

    def side_by_side(indices, width):
        row, col = iotas(comp, width)
        value = None
        for i, index in enumerate(indices):
            term = jnp.dot(total[index].astype(BF), picks(col == row + i * comp), preferred_element_type=F32)
            value = term if value is None else value + term
        return value.astype(BF)

    out[0] = side_by_side([atom + i for i in range(2 * REACH + 1)], out.shape[2])


def coupling_matrices(ids, neighbours, coupling, skip, count, wait):
    atoms, slots, orb, _ = coupling.shape
    comp = orb * orb
    wide = (2 * REACH + 1) * comp
    blocks = jnp.transpose(coupling, (0, 2, 1, 3)).reshape(atoms, orb * slots, orb)
    return pl.pallas_call(
        functools.partial(coupling_kernel, slots, skip),
        grid=(count,),
        out_shape=(jax.ShapeDtypeStruct((count, comp, wide), BF), token()),
        in_specs=[smem(), smem(), pl.BlockSpec((1, orb * slots, orb), lambda a: (a + skip, 0, 0)), anywhere()],
        out_specs=(pl.BlockSpec((1, comp, wide), lambda a: (a, 0, 0)), pl.BlockSpec(token().shape, lambda a: (0, 0))),
        scratch_shapes=[pltpu.VMEM((atoms + 2 * REACH, comp, comp), F32)],
        compiler_params=params(),
        cost_estimate=cost(0, 0),
    )(ids, neighbours, blocks, wait)


def edge_kernel(nz, ids, *refs):
    pieces, low, high = refs[:nz], refs[-2], refs[-1]
    for r in range(nz):
        turn = lax.rem(ids[0] + nz - r, nz)
        for j in range(2 * REACH):
            target = low if j < REACH else high

            @pl.when(turn == j)
            def _(r=r, j=j, target=target):
                target[j % REACH] = pieces[r][...]


def edge_pack(ids, pieces, waits):
    nz = len(pieces)
    out = jax.ShapeDtypeStruct((REACH,) + pieces[0].shape, BF)
    return pl.pallas_call(
        functools.partial(edge_kernel, nz),
        out_shape=(out, out),
        in_specs=[smem()] + [vmem()] * nz + [anywhere()] * len(waits),
        out_specs=(vmem(), vmem()),
        compiler_params=params(),
        cost_estimate=cost(0, nz * pieces[0].size * 4),
    )(ids, *pieces, *waits)


def arrive_kernel(*refs):
    refs[-1][...] = jnp.zeros_like(refs[-1])


def arrive(pieces):
    return pl.pallas_call(
        arrive_kernel,
        out_shape=token(),
        in_specs=[anywhere()] * len(pieces),
        out_specs=vmem(),
        compiler_params=params(),
        cost_estimate=pl.CostEstimate(flops=55 * 10**8, bytes_accessed=0, transcendentals=0),
    )(*pieces)


def apply_kernel(nz, c, ids, before, low, high, after, *refs):
    pieces, (below, above, _, out, held, ready, sems) = refs[:-7], refs[-7:]
    k, atoms, comps, energies = out.shape
    comp = comps // 2
    deep = below.shape[1]
    half = atoms // 2
    copies = []
    rows = pl.ds(c * comp, comp)
    for kk in range(0, k, 2):
        for b in range(2):
            cols = pl.ds(b * energies, energies)
            for j in range(REACH):
                for ref, at in ((before, j), (low, REACH + j), (high, atoms + j), (after, atoms + REACH + j)):
                    held[at * comp:(at + 1) * comp, cols] = ref[j, kk + b, rows, :]
            for i, piece in enumerate(pieces):
                at = (2 * REACH + i // nz * nz + lax.rem(ids[0] + nz - i % nz, nz)) * comp
                held[pl.ds(pl.multiple_of(at, 16), comp), cols] = piece[kk + b]
        for atom in range(atoms):
            matrix, at = (below, atom) if atom < half else (above, atom - half)
            value = jnp.dot(matrix[at * comp:(at + 1) * comp, :], held[atom * comp:atom * comp + deep, :], preferred_element_type=F32)
            for b in range(2):
                ready[kk + b, atom] = value[:, b * energies:(b + 1) * energies]
            block = (pl.ds(kk, 2), atom)
            copies.append(pltpu.make_async_copy(ready.at[block], out.at[(*block, rows)], sems.at[len(copies)]))
            copies[-1].start()
    for copy in copies:
        copy.wait()


def apply_couplings(ids, nz, c, before, low, high, after, pieces, below, above, wait, shape):
    k, atoms, comps, energies = shape
    comp = comps // 2
    matrices = [m.reshape(-1, m.shape[2]) for m in (below, above)]
    return pl.pallas_call(
        functools.partial(apply_kernel, nz, c),
        out_shape=jax.ShapeDtypeStruct(shape, F32),
        in_specs=[smem()] + [vmem()] * (4 + len(pieces) + len(matrices)) + [anywhere()],
        out_specs=anywhere(),
        scratch_shapes=[
            pltpu.VMEM(((atoms + 2 * REACH) * comp, 2 * energies), BF),
            pltpu.VMEM((k, atoms, comp, energies), F32),
            pltpu.SemaphoreType.DMA((k * atoms // 2,)),
        ],
        input_output_aliases={5 + len(pieces) + len(matrices): 0} if wait.shape == shape else {},
        compiler_params=params(),
        cost_estimate=cost(0, 0),
    )(ids, before, low, high, after, *pieces, *matrices, wait)


def shards(green, neighbours, offsets, emit_weight, absorb_weight, coupling):
    k, atoms, comps, energies = green.shape
    nz, ne, ny = (lax.axis_size(axis) for axis in ("momentum", "energy", "atom"))
    groups = atoms // nz
    ids = jnp.stack([lax.axis_index("momentum"), lax.axis_index("energy"), lax.axis_index("atom") * atoms]).astype(jnp.int32)
    green, ids = lax.optimization_barrier((green, ids))

    def around(array, r):
        return lax.ppermute(array, "momentum", [(i, (i + r) % nz) for i in range(nz)])

    if ne == 2:
        routes = [[(0, 1), (1, 0)]]
    else:
        routes = [[(i, i + 1) for i in range(ne - 1)], [(i + 1, i) for i in range(ne - 1)]]
    sides = len(routes)

    def send(group, *waits):
        if group == 0:
            sent = [lax.dynamic_index_in_dim(green, atom_of(group * nz + lax.rem(ids[0] + r, nz), atoms), 1, keepdims=False) for r in range(nz)]
        else:
            sent = pack(ids, green, nz, group, waits)
        return spread(sent, range(1, nz))

    def spread(sent, order):
        there = {r: around(sent[r], r) for r in order}
        return [sent[0]] + [there[r] for r in range(1, nz)]

    got = [send(0)]
    half = atoms // 2
    below, done = coupling_matrices(ids, neighbours, coupling, 0, half, got[0][0])
    above, done = coupling_matrices(ids, neighbours, coupling, half, half, done)

    main, *edges, done = tables(offsets, emit_weight, absorb_weight, ids, sides, nz, k, energies, done)
    for group in range(1, groups):
        got.append(send(group, done))
    waits = [done]
    back = []
    for group in range(groups):
        halos = halo_pack(ids, got[group], sides, waits)
        halos = [lax.ppermute(h, "energy", routes[i // 2]) for i, h in enumerate(halos)]
        parts = 1 if group == 0 else 2
        *sums, sum_done = phonon_sum(got[group], halos, main, edges, parts, [back[-1][0][r] for r in [nz // 2]] if back else [got[1][nz - 1]])
        waits = [sum_done]
        back.append([spread(sums[i::parts], range(1, nz)) for i in range(parts)])

    low, high = edge_pack(ids, back[0][0], waits)
    after = lax.ppermute(low, "atom", [(i + 1, i) for i in range(ny - 1)])
    before = lax.ppermute(high, "atom", [(i, i + 1) for i in range(ny - 1)])
    out = arrive([p for parts in back[1:] for p in parts[0][1:]])
    for c in range(2):
        pieces = [piece for parts in back[1:] for piece in parts[c]]
        out = apply_couplings(ids, nz, c, before, low, high, after, pieces, below, above, out, green.shape)
    return out


def solution(mesh):
    in_specs = (
        P("momentum", "atom", None, "energy"),
        P("atom", None),
        P(),
        P(),
        P(),
        P("atom", None, None, None),
    )
    out_specs = P("momentum", "atom", None, "energy")
    return jax.shard_map(shards, mesh=mesh, in_specs=in_specs, out_specs=out_specs, check_vma=False)
```

```python
import functools

import jax
import jax.numpy as jnp
from jax import lax
from jax.experimental import pallas as pl
from jax.experimental.pallas import tpu as pltpu
from jax.sharding import PartitionSpec as P

SMAX = 32
REACH = 2
BF = jnp.bfloat16
F32 = jnp.float32
VMEM_LIMIT = 16 * 1024 * 1024
PACK_LIMIT = 62 * 1024 * 1024


def params(limit=VMEM_LIMIT):
    return pltpu.CompilerParams(vmem_limit_bytes=limit)


def smem():
    return pl.BlockSpec(memory_space=pltpu.SMEM)


def vmem():
    return pl.BlockSpec(memory_space=pltpu.VMEM)


def anywhere():
    return pl.BlockSpec(memory_space=pl.ANY)


def token():
    return jax.ShapeDtypeStruct((8, 128), F32)


def cost(flops, nbytes):
    return pl.CostEstimate(flops=0, bytes_accessed=0, transcendentals=0)


def atom_of(turn, atoms):
    return jnp.where(turn < REACH, turn, jnp.where(turn < 2 * REACH, turn + atoms - 2 * REACH, turn - REACH))


def pack_kernel(group, nz, ids, green, *refs):
    outs, sems = refs[-nz - 1:-1], refs[-1]
    atoms = green.shape[1]
    copies = []
    for r in range(nz):
        atom = atom_of(group * nz + lax.rem(ids[0] + r, nz), atoms)
        copies.append(pltpu.make_async_copy(green.at[:, atom], outs[r], sems.at[r]))
    for copy in copies:
        copy.start()
    for copy in copies:
        copy.wait()


def pack(ids, green, nz, group, waits):
    k, _, comps, energies = green.shape
    piece = jax.ShapeDtypeStruct((k, comps, energies), BF)
    return pl.pallas_call(
        functools.partial(pack_kernel, group, nz),
        out_shape=(piece,) * nz,
        in_specs=[smem(), pl.BlockSpec(memory_space=pltpu.HBM)] + [vmem()] * len(waits),
        out_specs=(anywhere(),) * nz,
        scratch_shapes=[pltpu.SemaphoreType.DMA((nz,))],
        compiler_params=params(VMEM_LIMIT if waits else PACK_LIMIT),
        cost_estimate=cost(0, nz * piece.size * 4),
    )(ids, green, *waits)


def own_edge(place, side, sides, energies):
    last = place == 0 if sides == 1 else side == 0
    return jnp.where(last, energies - SMAX, 0)


def far_edge(place, side, sides, energies):
    above = place == 0 if sides == 1 else side == 1
    return jnp.where(above, energies, -SMAX)


def halo_kernel(nz, sides, ids, *refs):
    pieces, outs = refs[:nz], refs[-2 * sides:]
    half = nz // 2
    k, rows, energies = pieces[0].shape
    lanes = k * SMAX
    row = lax.broadcasted_iota(jnp.int32, (energies, lanes), 0)
    col = lax.broadcasted_iota(jnp.int32, (energies, lanes), 1)
    for side in range(sides):
        base = own_edge(ids[1], side, sides, energies)
        picks = [(row - base == col - kk * SMAX) & (col >= kk * SMAX) & (col < (kk + 1) * SMAX) for kk in range(k)]
        pick = jnp.concatenate([jnp.where(p, 1.0, 0.0) for p in picks], axis=0).astype(BF)
        for r in range(nz):
            wide = jnp.concatenate([pieces[r][kk] for kk in range(k)], axis=1)
            outs[2 * side + r // half][r % half] = jnp.dot(wide, pick, preferred_element_type=F32).astype(BF)


def halo_pack(ids, pieces, sides, waits):
    nz = len(pieces)
    k, rows, energies = pieces[0].shape
    out = jax.ShapeDtypeStruct((nz // 2, rows, k * SMAX), BF)
    return pl.pallas_call(
        functools.partial(halo_kernel, nz, sides),
        out_shape=(out,) * (2 * sides),
        in_specs=[smem()] + [vmem()] * nz + [anywhere()] * len(waits),
        out_specs=(vmem(),) * (2 * sides),
        compiler_params=params(),
        cost_estimate=cost(2 * sides * out.size * k * energies, nz * pieces[0].size * 2),
    )(ids, *pieces, *waits)


def table_kernel(nz, k, energies, sides, off_ref, emit_ref, absorb_ref, ids, _, *refs):
    main, halos, done, own, edge = refs[0], refs[1:1 + sides], refs[1 + sides], refs[2 + sides], refs[3 + sides]
    done[...] = jnp.zeros_like(done)
    phonons = off_ref.shape[0]
    total = nz * k
    pairs = total // 2

    def lag_matrix(lag, sources, first):
        distance = lax.broadcasted_iota(jnp.int32, (sources, energies), 1) - lax.broadcasted_iota(jnp.int32, (sources, energies), 0) - first
        value = jnp.zeros((sources, energies), F32)
        for w in range(phonons):
            value = jnp.where(distance == off_ref[w], emit_ref[w, lag], value)
            value = jnp.where(distance == -off_ref[w], absorb_ref[w, lag], value)
        return value.astype(BF)

    def step(lag, carry):
        own[lag] = lag_matrix(lag, energies, 0)
        for side in range(sides):
            edge[side, lag] = lag_matrix(lag, SMAX, far_edge(ids[1], side, sides, energies))
        return carry

    lax.fori_loop(0, total, step, 0)
    for i in range(2 * pairs - 1):
        m = 2 * (pairs - 1 - i)
        for a in range(2):
            for b in range(2):
                at = i * 2 * energies + a * energies
                main[at:at + energies, b * energies:(b + 1) * energies] = own[(m + b - a) % total]
    per = k // 2
    for side in range(sides):
        for par in range(per):
            for i in range(2 * nz - 1):
                m = 2 * (per * (nz - 1 - i) + par)
                for a in range(k):
                    for b in range(2):
                        at = i * k * SMAX + a * SMAX
                        halos[side][par, at:at + SMAX, b * energies:(b + 1) * energies] = edge[side, (m + b - a) % total]


def tables(offsets, emit, absorb, ids, sides, nz, k, energies, wait):
    total = nz * k
    main = jax.ShapeDtypeStruct(((total - 1) * 2 * energies, 2 * energies), BF)
    halo = jax.ShapeDtypeStruct((k // 2, (2 * nz - 1) * k * SMAX, 2 * energies), BF)
    return pl.pallas_call(
        functools.partial(table_kernel, nz, k, energies, sides),
        out_shape=(main,) + (halo,) * sides + (token(),),
        in_specs=[smem()] * 4 + [anywhere()],
        out_specs=(vmem(),) * (2 + sides),
        scratch_shapes=[pltpu.VMEM((total, energies, energies), BF), pltpu.VMEM((sides, total, SMAX, energies), BF)],
        compiler_params=params(),
        cost_estimate=cost(total * energies * energies * 100, main.size * 2),
    )(offsets, emit.astype(F32), absorb.astype(F32), ids, wait)


def sum_kernel(nz, sides, parts, *refs):
    pieces, refs = refs[:nz], refs[nz:]
    halos, refs = refs[:2 * sides], refs[2 * sides:]
    main, refs = refs[0], refs[1:]
    edges, refs = refs[:sides], refs[sides:]
    outs, done, wide = refs[-nz * parts - 2:-2], refs[-2], refs[-1]
    done[...] = jnp.zeros_like(done)
    k, rows, energies = pieces[0].shape
    total = nz * k
    pairs = total // 2
    per = k // 2
    strip = k * SMAX
    inner = total * energies
    for q in range(nz):
        piece = pieces[(nz - q) % nz]
        for kk in range(k):
            wide[:, (q * k + kk) * energies:(q * k + kk + 1) * energies] = piece[kk]
        for side in range(sides):
            at = inner + (side * nz + q) * strip
            r = (nz - q) % nz
            wide[:, at:at + strip] = halos[2 * side + r // (nz // 2)][r % (nz // 2)]
    for pair in range(pairs):
        top = (pairs - 1 - pair) * 2 * energies
        value = jnp.dot(wide[:, :inner], main[top:top + inner, :], preferred_element_type=F32)
        for side in range(sides):
            at = inner + side * nz * strip
            start = (nz - 1 - pair // per) * strip
            value += jnp.dot(wide[:, at:at + nz * strip], edges[side][pair % per, start:start + nz * strip, :], preferred_element_type=F32)
        value = value.astype(BF)
        size = rows // parts
        for i in range(parts):
            for b in range(2):
                outs[pair // per * parts + i][2 * (pair % per) + b] = value[i * size:(i + 1) * size, b * energies:(b + 1) * energies]


def phonon_sum(pieces, halos, main, edges, parts, waits):
    nz, sides = len(pieces), len(halos) // 2
    k, rows, energies = pieces[0].shape
    out = jax.ShapeDtypeStruct((k, rows // parts, energies), BF)
    depth = nz * k * energies + sides * nz * k * SMAX
    return pl.pallas_call(
        functools.partial(sum_kernel, nz, sides, parts),
        out_shape=(out,) * (nz * parts) + (token(),),
        in_specs=[vmem()] * (nz + 2 * sides + 1 + sides) + [anywhere()] * len(waits),
        out_specs=(vmem(),) * (nz * parts + 1),
        scratch_shapes=[pltpu.VMEM((rows, depth), BF)],
        compiler_params=params(),
        cost_estimate=cost(2 * rows * depth * nz * k * energies, main.size * 2),
    )(*pieces, *halos, main, *edges, *waits)


def coupling_kernel(slots, skip, ids, near_ref, c_ref, wait, out, done, total):
    atom = pl.program_id(0) + skip
    done[...] = jnp.zeros_like(done)
    blocks = c_ref[0]
    depth, orb = blocks.shape
    comp = total.shape[1]

    def iotas(rows, cols):
        return lax.broadcasted_iota(jnp.int32, (rows, cols), 0), lax.broadcasted_iota(jnp.int32, (rows, cols), 1)

    def picks(condition):
        return jnp.where(condition, 1.0, 0.0).astype(BF)

    def over(index):
        return lax.shift_right_logical(index * (4096 // orb + 1), 12)

    row, col = iotas(orb, comp)
    left = jnp.dot(blocks, picks(row == over(col)), preferred_element_type=F32).astype(BF)
    right = jnp.dot(blocks, picks(row == col - over(col) * orb), preferred_element_type=F32).astype(BF)
    total[...] = jnp.zeros_like(total)
    row, col = iotas(comp, depth)
    for n in range(slots):
        spread_left = jnp.dot(picks(col == over(row) * slots + n), left, preferred_element_type=F32)
        spread_right = jnp.dot(picks(col == (row - over(row) * orb) * slots + n), right, preferred_element_type=F32)
        total[near_ref[atom, n] - ids[2] + REACH] += spread_left * spread_right

    def side_by_side(indices, width):
        row, col = iotas(comp, width)
        value = None
        for i, index in enumerate(indices):
            term = jnp.dot(total[index].astype(BF), picks(col == row + i * comp), preferred_element_type=F32)
            value = term if value is None else value + term
        return value.astype(BF)

    out[0] = side_by_side([atom + i for i in range(2 * REACH + 1)], out.shape[2])


def coupling_matrices(ids, neighbours, coupling, skip, count, wait):
    atoms, slots, orb, _ = coupling.shape
    comp = orb * orb
    wide = (2 * REACH + 1) * comp
    blocks = jnp.transpose(coupling, (0, 2, 1, 3)).reshape(atoms, orb * slots, orb)
    return pl.pallas_call(
        functools.partial(coupling_kernel, slots, skip),
        grid=(count,),
        out_shape=(jax.ShapeDtypeStruct((count, comp, wide), BF), token()),
        in_specs=[smem(), smem(), pl.BlockSpec((1, orb * slots, orb), lambda a: (a + skip, 0, 0)), anywhere()],
        out_specs=(pl.BlockSpec((1, comp, wide), lambda a: (a, 0, 0)), pl.BlockSpec(token().shape, lambda a: (0, 0))),
        scratch_shapes=[pltpu.VMEM((atoms + 2 * REACH, comp, comp), F32)],
        compiler_params=params(),
        cost_estimate=cost(0, 0),
    )(ids, neighbours, blocks, wait)


def edge_kernel(nz, ids, *refs):
    pieces, low, high = refs[:nz], refs[-2], refs[-1]
    for r in range(nz):
        turn = lax.rem(ids[0] + nz - r, nz)
        for j in range(2 * REACH):
            target = low if j < REACH else high

            @pl.when(turn == j)
            def _(r=r, j=j, target=target):
                target[j % REACH] = pieces[r][...]


def edge_pack(ids, pieces, waits):
    nz = len(pieces)
    out = jax.ShapeDtypeStruct((REACH,) + pieces[0].shape, BF)
    return pl.pallas_call(
        functools.partial(edge_kernel, nz),
        out_shape=(out, out),
        in_specs=[smem()] + [vmem()] * nz + [anywhere()] * len(waits),
        out_specs=(vmem(), vmem()),
        compiler_params=params(),
        cost_estimate=cost(0, nz * pieces[0].size * 4),
    )(ids, *pieces, *waits)


def arrive_kernel(*refs):
    refs[-1][...] = jnp.zeros_like(refs[-1])


def arrive(pieces):
    return pl.pallas_call(
        arrive_kernel,
        out_shape=token(),
        in_specs=[anywhere()] * len(pieces),
        out_specs=vmem(),
        compiler_params=params(),
        cost_estimate=pl.CostEstimate(flops=55 * 10**8, bytes_accessed=0, transcendentals=0),
    )(*pieces)


def apply_kernel(nz, c, ids, before, low, high, after, *refs):
    pieces, (below, above, _, out, held, ready, sems) = refs[:-7], refs[-7:]
    k, atoms, comps, energies = out.shape
    comp = comps // 2
    deep = below.shape[1]
    half = atoms // 2
    copies = []
    rows = pl.ds(c * comp, comp)
    for kk in range(0, k, 2):
        for b in range(2):
            cols = pl.ds(b * energies, energies)
            for j in range(REACH):
                for ref, at in ((before, j), (low, REACH + j), (high, atoms + j), (after, atoms + REACH + j)):
                    held[at * comp:(at + 1) * comp, cols] = ref[j, kk + b, rows, :]
            for i, piece in enumerate(pieces):
                at = (2 * REACH + i // nz * nz + lax.rem(ids[0] + nz - i % nz, nz)) * comp
                held[pl.ds(pl.multiple_of(at, 16), comp), cols] = piece[kk + b]
        for atom in range(atoms):
            matrix, at = (below, atom) if atom < half else (above, atom - half)
            value = jnp.dot(matrix[at * comp:(at + 1) * comp, :], held[atom * comp:atom * comp + deep, :], preferred_element_type=F32)
            for b in range(2):
                ready[kk + b, atom] = value[:, b * energies:(b + 1) * energies]
            block = (pl.ds(kk, 2), atom)
            copies.append(pltpu.make_async_copy(ready.at[block], out.at[(*block, rows)], sems.at[len(copies)]))
            copies[-1].start()
    for copy in copies:
        copy.wait()


def apply_couplings(ids, nz, c, before, low, high, after, pieces, below, above, wait, shape):
    k, atoms, comps, energies = shape
    comp = comps // 2
    matrices = [m.reshape(-1, m.shape[2]) for m in (below, above)]
    return pl.pallas_call(
        functools.partial(apply_kernel, nz, c),
        out_shape=jax.ShapeDtypeStruct(shape, F32),
        in_specs=[smem()] + [vmem()] * (4 + len(pieces) + len(matrices)) + [anywhere()],
        out_specs=anywhere(),
        scratch_shapes=[
            pltpu.VMEM(((atoms + 2 * REACH) * comp, 2 * energies), BF),
            pltpu.VMEM((k, atoms, comp, energies), F32),
            pltpu.SemaphoreType.DMA((k * atoms // 2,)),
        ],
        input_output_aliases={5 + len(pieces) + len(matrices): 0} if wait.shape == shape else {},
        compiler_params=params(),
        cost_estimate=cost(0, 0),
    )(ids, before, low, high, after, *pieces, *matrices, wait)


def shards(green, neighbours, offsets, emit_weight, absorb_weight, coupling):
    k, atoms, comps, energies = green.shape
    nz, ne, ny = (lax.axis_size(axis) for axis in ("momentum", "energy", "atom"))
    groups = atoms // nz
    ids = jnp.stack([lax.axis_index("momentum"), lax.axis_index("energy"), lax.axis_index("atom") * atoms]).astype(jnp.int32)
    green, ids = lax.optimization_barrier((green, ids))

    def around(array, r):
        return lax.ppermute(array, "momentum", [(i, (i + r) % nz) for i in range(nz)])

    if ne == 2:
        routes = [[(0, 1), (1, 0)]]
    else:
        routes = [[(i, i + 1) for i in range(ne - 1)], [(i + 1, i) for i in range(ne - 1)]]
    sides = len(routes)

    def send(group, *waits):
        if group == 0:
            sent = [lax.dynamic_index_in_dim(green, atom_of(group * nz + lax.rem(ids[0] + r, nz), atoms), 1, keepdims=False) for r in range(nz)]
        else:
            sent = pack(ids, green, nz, group, waits)
        return spread(sent, range(1, nz))

    def spread(sent, order):
        there = {r: around(sent[r], r) for r in order}
        return [sent[0]] + [there[r] for r in range(1, nz)]

    got = [send(0)]
    half = atoms // 2
    below, done = coupling_matrices(ids, neighbours, coupling, 0, half, got[0][0])
    above, done = coupling_matrices(ids, neighbours, coupling, half, half, done)

    for group in range(1, groups):
        got.append(send(group, done))
    main, *edges, done = tables(offsets, emit_weight, absorb_weight, ids, sides, nz, k, energies, done)
    waits = [done]
    back = []
    for group in range(groups):
        halos = halo_pack(ids, got[group], sides, waits)
        halos = [lax.ppermute(h, "energy", routes[i // 2]) for i, h in enumerate(halos)]
        parts = 1 if group == 0 else 2
        *sums, sum_done = phonon_sum(got[group], halos, main, edges, parts, [back[-1][0][r] for r in [nz // 2]] if back else [got[1][nz - 1]])
        waits = [sum_done]
        back.append([spread(sums[i::parts], range(1, nz)) for i in range(parts)])

    low, high = edge_pack(ids, back[0][0], waits)
    after = lax.ppermute(low, "atom", [(i + 1, i) for i in range(ny - 1)])
    before = lax.ppermute(high, "atom", [(i, i + 1) for i in range(ny - 1)])
    out = arrive([p for parts in back[1:] for p in parts[0][1:]])
    for c in range(2):
        pieces = [piece for parts in back[1:] for piece in parts[c]]
        out = apply_couplings(ids, nz, c, before, low, high, after, pieces, below, above, out, green.shape)
    return out


def solution(mesh):
    in_specs = (
        P("momentum", "atom", None, "energy"),
        P("atom", None),
        P(),
        P(),
        P(),
        P("atom", None, None, None),
    )
    out_specs = P("momentum", "atom", None, "energy")
    return jax.shard_map(shards, mesh=mesh, in_specs=in_specs, out_specs=out_specs, check_vma=False)
```
